128 devices in a mesh: boards: 16 (over x, z), seq: 4 (over y), hand: 2 (over core).
Axes of the slice: x: 4, y: 4, z: 4, core: 2. Of those that a mesh axis runs over, the one named last changes fastest.
Arguments:
- board_cards: int32 [512, 5], P('boards'), may hold values from 0 to 51, as said below
- ranks: int32 [512, 1326], P('boards'), may hold values from 0 to 7461
- buckets: int32 [512, 1326], P('boards'), may hold values from 0 to 16383, as said below
- parent: int32 [64], replicated, may hold values from -1 to 31, as said below
- action: int32 [64], replicated, may hold values from 0 to 2
- pot: int32 [64], replicated, may hold values from 1 to 9
- logits: float32 [64, 16384], P('seq', ('boards', 'hand')), may hold values from -8 to 406
Outputs:
- new_logits: float32 [64, 16384], P('seq', ('boards', 'hand'))
- values: float32 [2, 64, 16384], P(None, 'seq', ('boards', 'hand'))
The draws below stay inside these ranges and needn't reach their ends.
Inputs may be any that keep to these rules, and one draw needn't show every extreme that they name: `board_cards`: each row holds five different cards of 0 to 51. All buckets of one board lie in one aligned window of 1024 buckets: buckets[b, h] // 1024 is the same for every hand h of board b. parent[0] = -1 and for s > 0 parent[s] lies between (s - 1) // 4 and (s - 1) // 2, so that the tree is at most 6 deep.
All inputs are finite; a program needn't handle non-finite values.
Results may differ from the reference program's by a relative error of at most 0.0003.
Values may be sent and summed in bfloat16 or wider, within the bound.
No kernel may reach another device: no remote copies, remote signals or barrier semaphores. Data moves between devices by JAX's collectives and lax.ppermute only.
A program may use at most 128 MiB of HBM per device.

```python
import jax
import jax.numpy as jnp
import numpy as np
from jax import lax

CARDS = 52
H = 1326
RANKS = 7462
S = 64
NBUCK = 16384
WIN = 1024
DEPTH = 6
BOARDS = 512


def draw_board_cards(key, part):
    key = jax.random.fold_in(key, 11)
    scores = jax.random.randint(key, (BOARDS, CARDS), 0, 1 << 20) * CARDS + jnp.arange(CARDS, dtype=jnp.int32)[None, :]
    order = jnp.argsort(scores, axis=1, stable=True)
    return order[:, :5].astype(jnp.int32)


def draw_buckets(key, part):
    key = jax.random.fold_in(key, 47)
    cluster_key, inner_key = jax.random.split(key)
    cluster = jax.random.randint(cluster_key, (BOARDS, 1), 0, NBUCK // WIN)
    inner = jax.random.randint(inner_key, (BOARDS, H), 0, WIN)
    return (cluster * WIN + inner).astype(jnp.int32)


def draw_parent(key, part):
    key = jax.random.fold_in(key, 23)
    index = jnp.arange(S, dtype=jnp.int32)
    lower = jnp.maximum(index - 1, 0) // 4
    upper = jnp.maximum(index - 1, 0) // 2
    picks = jax.random.randint(key, (S,), 0, 1 << 20)
    chosen = lower + picks % (upper - lower + 1)
    chosen = jnp.where(index == S - 1, upper, chosen)
    return jnp.where(index == 0, -1, chosen).astype(jnp.int32)


def draw_logits(key, part):
    key = jax.random.fold_in(key, 37)
    first_key = jax.random.fold_in(key, 0)
    return jnp.clip(2.0 * jax.random.normal(first_key, (S, NBUCK), jnp.float32), -8.0, 8.0)


def touch_ends(result, key, smallest, top_value):
    index_at = [jax.random.randint(jax.random.fold_in(key, axis), (), 0, length) for axis, length in enumerate(result.shape)]
    widest = result.shape.index(max(result.shape))
    beside = index_at[:widest] + [(index_at[widest] + 1) % result.shape[widest]] + index_at[widest + 1:]
    return result.at[tuple(index_at)].set(smallest).at[tuple(beside)].set(top_value)


def setup_inputs(seed: int = 0) -> dict:
    key_list = jax.random.split(jax.random.key(seed), 8)
    return {
        "board_cards": draw_board_cards(jax.random.fold_in(key_list[7], 71), 0),
        "ranks": touch_ends(jax.random.randint(key_list[1], (BOARDS, H), 0, RANKS), jax.random.fold_in(key_list[1], 1), 0, RANKS - 1).astype(jnp.int32),
        "buckets": draw_buckets(jax.random.fold_in(key_list[7], 71), 0),
        "parent": draw_parent(jax.random.fold_in(key_list[7], 71), 0),
        "action": touch_ends(jax.random.randint(key_list[4], (S,), 0, 3), jax.random.fold_in(key_list[4], 1), 0, 2).astype(jnp.int32),
        "pot": touch_ends(jax.random.randint(key_list[5], (S,), 1, 10), jax.random.fold_in(key_list[5], 1), 1, 9).astype(jnp.int32),
        "logits": draw_logits(jax.random.fold_in(key_list[7], 71), 0),
    }


STEP = 0.5


def hand_cards():
    first, second = np.triu_indices(CARDS, 1)
    return jnp.asarray(first, dtype=jnp.int32), jnp.asarray(second, dtype=jnp.int32)


def tree_tables(parent, action):
    index = jnp.arange(S, dtype=jnp.int32)
    safe = jnp.maximum(parent, 0)
    depth = jnp.zeros((S,), jnp.int32)
    for level in range(DEPTH):
        depth = jnp.where(index == 0, 0, jnp.take(depth, safe) + 1)
    actor = (depth + 1) % 2
    children = jnp.sum((parent[None, :] == index[:, None]).astype(jnp.int32), axis=1)
    show = (children == 0) & (action != 0)
    fold = (children == 0) & (action == 0)
    return safe, actor, show, fold


def policy(logits, parent):
    group = parent + 1
    top = jax.ops.segment_max(logits, group, num_segments=S + 1)
    shifted = jnp.exp(logits - jnp.take(top, group, axis=0))
    total = jax.ops.segment_sum(shifted, group, num_segments=S + 1)
    return shifted / jnp.take(total, group, axis=0)


def player_weights(sigma, actor):
    return jnp.stack([jnp.where((actor == player)[:, None], sigma, jnp.ones_like(sigma)) for player in range(2)])


def reach_of(weights, safe):
    index = jnp.arange(S, dtype=jnp.int32)[None, :, None]
    reach = jnp.ones_like(weights)
    for level in range(DEPTH):
        reach = jnp.where(index == 0, jnp.ones_like(weights), weights * jnp.take(reach, safe, axis=1))
    return reach


def backup(leaf_mean, weights, parent):
    values = leaf_mean
    for level in range(DEPTH):
        carried = jax.ops.segment_sum(jnp.moveaxis(weights * values, 1, 0), parent + 1, num_segments=S + 1)
        values = leaf_mean + jnp.moveaxis(carried[1:], 0, 1)
    return values


def advance(logits, values, safe, actor):
    index = jnp.arange(S, dtype=jnp.int32)[:, None]
    chooser = (actor == 0)[:, None]
    own_self = jnp.where(chooser, values[0], values[1])
    own_parent = jnp.where(chooser, jnp.take(values[0], safe, axis=0), jnp.take(values[1], safe, axis=0))
    gain = jnp.where(index == 0, jnp.zeros_like(own_self), own_self - own_parent)
    return logits + STEP * gain


def reference(board_cards, ranks, buckets, parent, action, pot, logits):
    safe, actor, show, fold = tree_tables(parent, action)
    sigma = policy(logits, parent)
    weights = player_weights(sigma, actor)
    reach_b = reach_of(weights, safe).astype(jnp.bfloat16)
    first, second = hand_cards()
    hands = first.shape[0]
    compat = ((first[:, None] != first[None, :]) & (first[:, None] != second[None, :])
              & (second[:, None] != first[None, :]) & (second[:, None] != second[None, :]))
    compat_b = compat.astype(jnp.bfloat16)
    compat_i = compat.astype(jnp.int32)
    scale = pot.astype(jnp.float32) / hands
    player = jnp.arange(2, dtype=jnp.int32)[:, None]
    fold_sign = jnp.where(actor[None, :] == player, -1.0, 1.0).astype(jnp.float32)

    def one_board(cards, rank, bucket):
        live = jnp.all(first[:, None] != cards[None, :], axis=1) & jnp.all(second[:, None] != cards[None, :], axis=1)
        live_f = live.astype(jnp.float32)
        against = (jnp.sign(rank[None, :] - rank[:, None]) * compat_i).astype(jnp.bfloat16)
        opponent = jnp.take(reach_b, bucket, axis=2) * live.astype(jnp.bfloat16)[None, None, :]
        opponent = opponent[::-1].reshape(2 * S, hands)
        show_val = jnp.dot(opponent, against, preferred_element_type=jnp.float32).reshape(2, S, hands)
        fold_val = jnp.dot(opponent, compat_b, preferred_element_type=jnp.float32).reshape(2, S, hands)
        chosen = jnp.where(show[None, :, None], show_val,
                           jnp.where(fold[None, :, None], fold_sign[:, :, None] * fold_val, jnp.zeros_like(fold_val)))
        terms = chosen * scale[None, :, None] * live_f[None, None, :]
        return terms.reshape(2 * S, hands).T, live_f

    block = 8
    count = board_cards.shape[0] // block

    def step(carry, pieces):
        sums, mass = carry
        cards, rank, bucket = pieces
        terms, live = jax.vmap(one_board)(cards, rank, bucket)
        sums = sums + jax.ops.segment_sum(terms.reshape(-1, 2 * S), bucket.reshape(-1), num_segments=NBUCK)
        mass = mass + jax.ops.segment_sum(live.reshape(-1), bucket.reshape(-1), num_segments=NBUCK)
        return (sums, mass), None

    initial = (jnp.zeros((NBUCK, 2 * S), jnp.float32), jnp.zeros((NBUCK,), jnp.float32))
    (sums, mass), unused = lax.scan(step, initial, (board_cards.reshape(count, block, 5),
                                                     ranks.reshape(count, block, hands),
                                                     buckets.reshape(count, block, hands)))
    mean = sums / (mass + 1.0)[:, None]
    leaf_mean = jnp.transpose(mean.reshape(NBUCK, 2, S), (1, 2, 0))
    values = backup(leaf_mean, weights, parent)
    new_logits = advance(logits, values, safe, actor)
    return new_logits, values
```

```python
import functools

import jax
import jax.numpy as jnp
import ml_dtypes
import numpy as np
from jax import lax
from jax.experimental import pallas as pl
from jax.experimental.pallas import tpu as pltpu
from jax.sharding import PartitionSpec as P

CARDS = 52
S = 64
WIN = 1024
H = CARDS * (CARDS - 1) // 2
HP = 1408
EXT = 256
DEAD = 2047
STEP = 0.5
BF = jnp.bfloat16
F32 = jnp.float32
VM = pl.BlockSpec(memory_space=pltpu.VMEM)
SM = pl.BlockSpec(memory_space=pltpu.SMEM)


def constants():
    first, second = np.triu_indices(CARDS, 1)
    pair = np.full((2, H), -1, np.int32)
    pair[0], pair[1] = first, second
    held = np.zeros((HP, 64), np.float32)
    held[np.arange(H), first] = 1
    held[np.arange(H), second] = 1
    share = held @ held.T
    compat = np.zeros((HP, HP), np.float32)
    compat[:H, :H] = share[:H, :H] == 0
    held[:H, CARDS] = 1
    gather = np.zeros((HP, EXT), np.float32)
    spread = np.zeros((EXT, HP), np.float32)
    for part in range(3):
        gather[:, 64 * part : 64 * part + 64] = held
        spread[64 * part : 64 * part + CARDS] = -held[:, :CARDS].T
        spread[64 * part + CARDS, :H] = 1
    k = np.arange(WIN)
    code = ((128 + k % 128) * 2.0 ** (k // 128))[None, :]
    cast = lambda a: np.asarray(a, ml_dtypes.bfloat16)
    return pair, cast(compat), cast(gather), cast(spread), cast(code)


def coded(value):
    power = jnp.ones(value.shape, F32)
    for bit in range(6):
        on = (value >> (7 + bit)) & 1
        power = power * jnp.where(on == 1, float(2 ** (2**bit)), 1.0)
    return ((value & 127) + 128).astype(F32) * power


def prep_kernel(plane_ref, cards_ref, ranks_ref, buckets_ref, pair_ref, out_ref):
    bucket = buckets_ref[...]
    cards = cards_ref[...]
    first, second = pair_ref[0:1, :], pair_ref[1:2, :]
    word = bucket & (WIN - 1)
    for c in range(5):
        card = cards[:, c : c + 1]
        word = jnp.where((first == card) | (second == card), DEAD, word)
    word = word + ranks_ref[...] * 65536
    boards = bucket.shape[0]
    cluster = bucket[:, 0:1] // WIN
    row = lax.broadcasted_iota(jnp.int32, (boards, boards), 0)
    col = lax.broadcasted_iota(jnp.int32, (boards, boards), 1)
    key = (cluster * boards + row[:, 0:1]).astype(F32)
    across = jnp.sum(jnp.where(row == col, key, 0.0), axis=0, keepdims=True)
    place = jnp.sum(jnp.where(across < key, 1.0, 0.0), axis=1, keepdims=True).astype(jnp.int32)
    plane = plane_ref[0]
    for t in range(out_ref.shape[0]):
        mine = place == 8 * t + plane
        home = jnp.sum(jnp.where(mine, cluster, 0), axis=0, keepdims=True) * 65536 + DEAD
        out_ref[t : t + 1, :] = jnp.broadcast_to(home, (1, HP))
        out_ref[t : t + 1, 0:H] = jnp.sum(jnp.where(mine, word, 0), axis=0, keepdims=True)


def tree_scalars(parent_ref, depth, inner):
    depth[0] = 0
    for s in range(S):
        inner[s] = 0
    for s in range(1, S):
        up = parent_ref[s]
        depth[s] = depth[up] + 1
        inner[up] = 1


def reach_kernel(
    place_ref, parent_ref, action_ref, *refs
):
    blocks = refs[:4]
    reach_ref, sigma_ref, show_ref, fold_ref = refs[4:8]
    line, top, reach, depth, inner = refs[8:]
    seq, hand = place_ref[0], place_ref[1]
    tree_scalars(parent_ref, depth, inner)
    for k in range(4):
        base = 128 * jnp.bitwise_xor(seq, k)
        for half in range(2):
            start = base + 4 * jnp.bitwise_xor(hand, half)
            for r in range(4):
                line[pl.ds(start + r, 16, stride=8), :] = blocks[k][half, :, 128 * r : 128 * r + 128]

    def at(s):
        return pl.ds(pl.multiple_of(8 * s, 8), 8)

    top[...] = jnp.full(top.shape, -jnp.inf, F32)
    for s in range(1, S):
        up = at(parent_ref[s])
        top[up, :] = jnp.maximum(top[up, :], line[8 * s : 8 * s + 8, :])
    for s in range(1, S):
        up = at(parent_ref[s])
        sigma_ref[8 * s : 8 * s + 8, :] = jnp.exp(line[8 * s : 8 * s + 8, :] - top[up, :])
    top[...] = jnp.zeros(top.shape, F32)
    for s in range(1, S):
        up = at(parent_ref[s])
        top[up, :] = top[up, :] + sigma_ref[8 * s : 8 * s + 8, :]
    one = jnp.ones((8, 128), F32)
    sigma_ref[0:8, :] = one
    for p in range(2):
        reach[p, 0:8, :] = one
    zero = jnp.zeros((1, 128), F32)
    show_ref[0:1, :] = zero
    show_ref[S : S + 1, :] = zero
    fold_ref[0:1, :] = zero
    fold_ref[S : S + 1, :] = zero
    for s in range(1, S):
        up = at(parent_ref[s])
        sigma = sigma_ref[8 * s : 8 * s + 8, :] / top[up, :]
        sigma_ref[8 * s : 8 * s + 8, :] = sigma
        actor = (depth[s] + 1) % 2
        for p in range(2):
            weight = jnp.where(actor == p, sigma, one)
            reach[p, 8 * s : 8 * s + 8, :] = weight * reach[p, up, :]
        leaf = 1 - inner[s]
        folds = jnp.where(action_ref[s] == 0, leaf, 0)
        shows = (leaf - folds).astype(F32)
        folds = folds.astype(F32)
        for p in range(2):
            show_ref[p * S + s : p * S + s + 1, :] = jnp.full((1, 128), shows, F32)
            sign = jnp.where(actor == p, -folds, folds)
            fold_ref[p * S + s : p * S + s + 1, :] = jnp.full((1, 128), sign, F32)
    for p in range(2):
        for r in range(8):
            reach_ref[p * S : p * S + S, 128 * r : 128 * r + 128] = reach[
                1 - p, pl.ds(r, S, stride=8), :
            ].astype(BF)


def pieces(width):
    return [(a, min(a + 256, width)) for a in range(0, width, 256)]


def board(row, reach_ref, show_ref, fold_ref, compat_ref, gather_ref, spread_ref, code_ref,
          sums, vcol, onehot, left, diag, terms):
    rank_row = coded(row >> 16)
    slot_row = coded(row & 65535)
    both = jnp.concatenate([rank_row, slot_row, jnp.zeros((6, HP), F32)], axis=0)
    for j in range(HP // 128):
        down = both[:, 128 * j : 128 * j + 128].T
        vcol[128 * j : 128 * j + 128, :] = jnp.broadcast_to(down[:, 0:1], (128, 128)).astype(BF)
        slot = jnp.broadcast_to(down[:, 1:2], (128, 128)).astype(BF)
        for t in range(WIN // 128):
            key = code_ref[0:1, 128 * t : 128 * t + 128]
            onehot[128 * j : 128 * j + 128, 128 * t : 128 * t + 128] = jnp.where(
                slot == key, jnp.ones((), BF), jnp.zeros((), BF)
            )
    rank_row = rank_row.astype(BF)
    show = show_ref[...].astype(BF)
    fold = fold_ref[...].astype(BF)
    for a, b in pieces(HP):
        spread = lax.dot_general(
            reach_ref[...], onehot[a:b, :], (((1,), (1,)), ((), ())), preferred_element_type=F32
        ).astype(BF)
        for c in range(a, b, 128):
            part = spread[:, c - a : c - a + 128]
            left[:, c : c + 128] = part * show
            diag[:, c : c + 128] = part * fold
    cards = jnp.dot(diag[...], gather_ref[...], preferred_element_type=F32)
    high = cards.astype(BF)
    rest = cards - high.astype(F32)
    middle = rest.astype(BF)
    low = (rest - middle.astype(F32)).astype(BF)
    lane = lax.broadcasted_iota(jnp.int32, cards.shape, 1)
    left[:, HP:] = jnp.where(lane < 64, high.astype(F32), jnp.where(lane < 128, middle.astype(F32), low.astype(F32))).astype(BF)
    for a, b in pieces(HP):
        limit = compat_ref[:, a:b]
        gap = rank_row[:, a:b] - jnp.concatenate([vcol[...]] * ((b - a) // 128), axis=1)
        against = jnp.minimum(jnp.maximum(gap, -limit), limit)
        chosen = jnp.dot(left[:, :HP], against, preferred_element_type=F32)
        chosen = chosen + jnp.dot(left[:, HP:], spread_ref[:, a:b], preferred_element_type=F32)
        chosen = chosen + diag[:, a:b].astype(F32)
        count = lax.broadcasted_iota(jnp.int32, chosen.shape, 0) == 0
        chosen = jnp.where(count, 1.0, chosen)
        high = chosen.astype(BF)
        terms[0 : 2 * S, a:b] = high
        terms[2 * S :, a:b] = (chosen - high.astype(F32)).astype(BF)
    for a, b in pieces(WIN):
        got = jnp.dot(terms[...], onehot[:, a:b], preferred_element_type=F32)
        sums[:, a:b] = sums[:, a:b] + got[: 2 * S] + got[2 * S :]


def board_kernel(
    home_ref, place_ref, parent_ref, pot_ref, b0, b1, b2, b3, reach_ref, sigma_ref, show_ref,
    fold_ref, compat_ref, gather_ref, spread_ref, code_ref, mine_ref, theirs_ref,
    sums, vcol, onehot, left, diag, terms, value, depth, inner,
):
    sums[...] = jnp.zeros(sums.shape, F32)
    me = place_ref[2]
    for index, block in enumerate((b0, b1, b2, b3)):

        def step(i, carry, index=index, block=block):
            @pl.when(home_ref[index * 16 + i] == me)
            def _():
                board(block[pl.ds(i, 1), :], reach_ref, show_ref, fold_ref, compat_ref, gather_ref,
                      spread_ref, code_ref, sums, vcol, onehot, left, diag, terms)

            return carry

        lax.fori_loop(0, 16, step, 0)
    tree_scalars(parent_ref, depth, inner)
    for p in range(2):
        for r in range(8):
            value[p, pl.ds(r, S, stride=8), :] = sums[p * S : p * S + S, 128 * r : 128 * r + 128]
    hand = place_ref[1]

    def at(s):
        return pl.ds(pl.multiple_of(8 * s, 8), 8)

    def put(rows, tile):
        turned = jnp.concatenate([tile[4:], tile[:4]], axis=0)
        tile = jnp.where(hand == 0, tile, turned)
        mine_ref[rows : rows + 4, :] = tile[:4]
        theirs_ref[rows : rows + 4, :] = tile[4:]

    put(3 * 4 * S, value[0, 0:8, :])
    mine_ref[3 * 4 * S + 4 :, :] = jnp.zeros((4, 128), F32)
    theirs_ref[3 * 4 * S + 4 :, :] = jnp.zeros((4, 128), F32)
    value[0, 0:8, :] = jnp.zeros((8, 128), F32)
    for s in range(1, S):
        scale = pot_ref[s].astype(F32) / H
        for p in range(2):
            value[p, 8 * s : 8 * s + 8, :] = value[p, 8 * s : 8 * s + 8, :] * scale
    for s in range(S - 1, 0, -1):
        up = at(parent_ref[s])
        sigma = sigma_ref[8 * s : 8 * s + 8, :]
        actor = (depth[s] + 1) % 2
        for p in range(2):
            own = value[p, 8 * s : 8 * s + 8, :]
            value[p, up, :] = value[p, up, :] + jnp.where(actor == p, sigma, 1.0) * own
    for s in range(S):
        for p in range(2):
            put(4 * (p * S + s), value[p, 8 * s : 8 * s + 8, :])
        if s == 0:
            put(4 * (2 * S + s), jnp.zeros((8, 128), F32))
        else:
            up = at(parent_ref[s])
            actor = (depth[s] + 1) % 2
            own = jnp.where(actor == 0, value[0, 8 * s : 8 * s + 8, :], value[1, 8 * s : 8 * s + 8, :])
            over = jnp.where(actor == 0, value[0, up, :], value[1, up, :])
            put(4 * (2 * S + s), own - over)


def chunk_kernel(place_ref, mine_ref, got_ref, *outs):
    seq = place_ref[0]
    for k in range(4):
        base = 64 * jnp.bitwise_xor(seq, k)
        for a in range(3):
            rows = pl.ds(pl.multiple_of(256 * a + base, 64), 64)
            outs[k][64 * a : 64 * a + 64, :] = mine_ref[rows, :] + got_ref[rows, :]
        outs[k][192:200, :] = mine_ref[768:776, :] + got_ref[768:776, :]


def finish_kernel(logits_ref, c0, c1, c2, c3, new_ref, values_ref, total):
    total[...] = (c0[...] + c1[...]) + (c2[...] + c3[...])
    for r in range(4):
        mass = total[192 + r : 193 + r, :] + 1.0
        lanes = slice(128 * r, 128 * r + 128)
        for p in range(2):
            values_ref[p, :, lanes] = total[pl.ds(64 * p + r, 16, stride=4), :] / mass
        gain = total[pl.ds(128 + r, 16, stride=4), :] / mass
        new_ref[:, lanes] = logits_ref[:, lanes] + STEP * gain


def swap(x, axis, size, bits):
    return lax.ppermute(x, axis, [(i, i ^ bits) for i in range(size)])


def local(board_cards, ranks, buckets, parent, action, pot, logits):
    sds = jax.ShapeDtypeStruct
    pair, compat, gather, spread, code = constants()
    b, q, h = (lax.axis_index(a) for a in ("boards", "seq", "hand"))
    plane = ((2 * q + h + b) % 8).astype(jnp.int32)[None]
    place = jnp.stack([q, h, b]).astype(jnp.int32)
    count = board_cards.shape[0] // 8
    own = pl.pallas_call(
        prep_kernel,
        out_shape=sds((count, HP), jnp.int32),
        in_specs=[SM, VM, VM, VM, VM],
        out_specs=VM,
    )(plane, board_cards, ranks, buckets, jnp.asarray(pair))
    other = swap(logits, "hand", 2, 1)
    wide = jnp.stack([logits, other])
    blocks = [wide] + [swap(wide, "seq", 4, k) for k in range(1, 4)]
    line = jnp.concatenate([own] + [swap(own, "boards", 16, 4 * k) for k in range(1, 4)], axis=0)
    packs = [line] + [swap(line, "boards", 16, k) for k in range(1, 4)]
    reach, sigma, show, fold = pl.pallas_call(
        reach_kernel,
        out_shape=[sds((2 * S, WIN), BF), sds((8 * S, 128), F32), sds((2 * S, 128), F32), sds((2 * S, 128), F32)],
        in_specs=[SM, SM, SM] + [VM] * 4,
        out_specs=[VM] * 4,
        scratch_shapes=[
            pltpu.VMEM((8 * S, 128), F32),
            pltpu.VMEM((8 * S, 128), F32),
            pltpu.VMEM((2, 8 * S, 128), F32),
            pltpu.SMEM((S,), jnp.int32),
            pltpu.SMEM((S,), jnp.int32),
        ],
        cost_estimate=pl.CostEstimate(flops=4_000_000, bytes_accessed=2_000_000, transcendentals=65536),
    )(place, parent, action, *blocks)
    home = jnp.concatenate([p[:, H] for p in packs]) // 65536
    mine, theirs = pl.pallas_call(
        board_kernel,
        out_shape=[sds((776, 128), F32)] * 2,
        in_specs=[SM] * 4 + [VM] * 12,
        out_specs=[VM] * 2,
        scratch_shapes=[
            pltpu.VMEM((2 * S, WIN), F32),
            pltpu.VMEM((HP, 128), BF),
            pltpu.VMEM((HP, WIN), BF),
            pltpu.VMEM((2 * S, HP + EXT), BF),
            pltpu.VMEM((2 * S, HP), BF),
            pltpu.VMEM((4 * S, HP), BF),
            pltpu.VMEM((2, 8 * S, 128), F32),
            pltpu.SMEM((S,), jnp.int32),
            pltpu.SMEM((S,), jnp.int32),
        ],
        compiler_params=pltpu.CompilerParams(vmem_limit_bytes=48 * 2**20),
        cost_estimate=pl.CostEstimate(flops=8_000_000_000, bytes_accessed=8_000_000, transcendentals=0),
    )(home, place, parent, pot, *packs, reach, sigma, show, fold,
      jnp.asarray(compat), jnp.asarray(gather), jnp.asarray(spread), jnp.asarray(code))
    got = swap(theirs, "hand", 2, 1)
    chunks = pl.pallas_call(
        chunk_kernel,
        out_shape=[sds((200, 128), F32)] * 4,
        in_specs=[SM, VM, VM],
        out_specs=[VM] * 4,
    )(place, mine, got)
    chunks = [chunks[0]] + [swap(chunks[k], "seq", 4, k) for k in range(1, 4)]
    new_logits, values = pl.pallas_call(
        finish_kernel,
        out_shape=[sds(logits.shape, F32), sds((2,) + logits.shape, F32)],
        in_specs=[VM] * 5,
        out_specs=[VM] * 2,
        scratch_shapes=[pltpu.VMEM((200, 128), F32)],
    )(logits, *chunks)
    return new_logits, values


def solution(mesh):
    return jax.shard_map(
        local,
        mesh=mesh,
        in_specs=(
            P("boards", None),
            P("boards", None),
            P("boards", None),
            P(),
            P(),
            P(),
            P("seq", ("boards", "hand")),
        ),
        out_specs=(P("seq", ("boards", "hand")), P(None, "seq", ("boards", "hand"))),
        check_vma=False,
    )
```

```python
import functools

import jax
import jax.numpy as jnp
import ml_dtypes
import numpy as np
from jax import lax
from jax.experimental import pallas as pl
from jax.experimental.pallas import tpu as pltpu
from jax.sharding import PartitionSpec as P

CARDS = 52
FREE = CARDS - 5
S = 64
WIN = 1024
H = CARDS * (CARDS - 1) // 2
LIVE = FREE * (FREE - 1) // 2
HQ = 1408
HP = 1152
EXT = 128
DEAD = 2047
STEP = 0.5
BF = jnp.bfloat16
F32 = jnp.float32
VM = pl.BlockSpec(memory_space=pltpu.VMEM)
SM = pl.BlockSpec(memory_space=pltpu.SMEM)
HB = pl.BlockSpec(memory_space=pltpu.HBM)


def constants():
    pair = np.full((2, HQ), CARDS, np.int32)
    pair[:, :H] = np.triu_indices(CARDS, 1)
    first, second = np.triu_indices(FREE, 1)
    held = np.zeros((HP, 64), np.float32)
    held[np.arange(LIVE), first] = 1
    held[np.arange(LIVE), second] = 1
    compat = np.zeros((HP, HP), np.float32)
    compat[:LIVE, :LIVE] = (held @ held.T)[:LIVE, :LIVE] == 0
    held[:LIVE, FREE] = 1
    gather = np.concatenate([held, held], axis=1)
    held[:, :FREE] *= -1
    spread = np.concatenate([held, held], axis=1).T
    k = np.arange(WIN)
    code = np.broadcast_to(((128 + k % 128) * 2.0 ** (k // 128))[:, None], (WIN, 128))
    cast = lambda a: np.asarray(a, ml_dtypes.bfloat16)
    return pair, cast(compat), cast(gather), cast(spread), cast(code)


def coded(value):
    power = jnp.ones(value.shape, F32)
    for bit in range(6):
        on = (value >> (7 + bit)) & 1
        power = power * jnp.where(on == 1, float(2 ** (2**bit)), 1.0)
    return ((value & 127) + 128).astype(F32) * power


def prep_kernel(cards_ref, ranks_ref, buckets_ref, pair_ref, out_ref, wide):
    boards = buckets_ref.shape[0]
    wide[:, 0:H] = ranks_ref[...] * 2048 + (buckets_ref[...] & (WIN - 1))
    lanes = lax.broadcasted_iota(jnp.int32, (1, HQ), 1)
    row = lax.broadcasted_iota(jnp.int32, (boards, boards), 0)
    col = lax.broadcasted_iota(jnp.int32, (boards, boards), 1)

    def across(key):
        return jnp.sum(jnp.where(row == col, key.astype(F32), 0.0), axis=0, keepdims=True)

    def down(key):
        return jnp.sum(jnp.where(row == col, key.astype(F32), 0.0), axis=1, keepdims=True).astype(jnp.int32)

    first, second = pair_ref[0:1, :], pair_ref[1:2, :]
    low, high = first, second
    dead = lanes >= H
    for c in range(5):
        card = down(cards_ref[c : c + 1, :])
        dead = dead | (first == card) | (second == card)
        low = low - jnp.where(card < first, 1, 0)
        high = high - jnp.where(card < second, 1, 0)
    shift = lanes - (((low * (2 * FREE - 1 - low)) >> 1) + high - low - 1)
    word = jnp.where(dead, DEAD, (wide[...] & 0xFFFFFF) + (shift << 24))
    for bit in range(8):
        moved = pltpu.roll(word, HQ - (1 << bit), 1)
        stays = ((word >> (24 + bit)) & 1) == 0
        word = jnp.where(((moved >> (24 + bit)) & 1) == 1, moved, jnp.where(stays, word, DEAD))
    word = jnp.where(lanes[:, :HP] < LIVE, word[:, :HP] & 0xFFFFFF, 2048 + DEAD)
    plane = 2 * lax.axis_index("seq") + lax.axis_index("hand")
    group = lax.axis_index("boards")
    cluster = buckets_ref[:, 0:1] // WIN
    twin = (across(cluster) == cluster.astype(F32)) & (col < row)
    twins = jnp.sum(jnp.where(twin, 1.0, 0.0), axis=1, keepdims=True).astype(jnp.int32)
    slots = out_ref.shape[1]
    slot = jnp.where(
        ((cluster + (group >> 1) + 4 * (group & 1) + twins) & 7) == plane, slots * cluster + (twins >> 3), -1
    )
    taken = lax.broadcasted_iota(jnp.int32, (slots * out_ref.shape[0], boards), 0).astype(F32) == across(slot)
    taken = jnp.where(taken, 1.0, 0.0).astype(BF)

    def deal(shift):
        part = ((word >> shift) & 255).astype(F32).astype(BF)
        return jnp.dot(taken, part, preferred_element_type=F32).astype(jnp.int32)

    word = deal(0) + (deal(8) << 8) + (deal(16) << 16)
    word = ((word >> 11) << 16) + (word & 2047)
    for c in range(out_ref.shape[0]):
        out_ref[c] = word[slots * c : slots * c + slots, :]


def tree_scalars(parent_ref, depth, inner):
    depth[0] = 0
    for s in range(S):
        inner[s] = 0
    for s in range(1, S):
        up = parent_ref[s]
        depth[s] = depth[up] + 1
        inner[up] = 1


def reach_kernel(parent_ref, action_ref, *refs):
    blocks = refs[:8]
    reach_ref, sigma_ref, show_ref, fold_ref, actor_ref = refs[8:13]
    line, top, reach, depth, inner = refs[13:]
    seq, hand = lax.axis_index("seq"), lax.axis_index("hand")
    tree_scalars(parent_ref, depth, inner)
    actor_ref[0] = 1
    for k in range(4):
        base = 128 * jnp.bitwise_xor(seq, k)
        for half in range(2):
            start = base + 4 * jnp.bitwise_xor(hand, half)
            for r in range(4):
                line[pl.ds(start + r, 16, stride=8), :] = blocks[4 * half + k][
                    :, 128 * r : 128 * r + 128
                ]

    def at(s):
        return pl.ds(pl.multiple_of(8 * s, 8), 8)

    top[...] = jnp.full(top.shape, -jnp.inf, F32)
    for s in range(1, S):
        up = at(parent_ref[s])
        top[up, :] = jnp.maximum(top[up, :], line[8 * s : 8 * s + 8, :])
    for s in range(1, S):
        up = at(parent_ref[s])
        sigma_ref[8 * s : 8 * s + 8, :] = jnp.exp(line[8 * s : 8 * s + 8, :] - top[up, :])
    top[...] = jnp.zeros(top.shape, F32)
    for s in range(1, S):
        up = at(parent_ref[s])
        top[up, :] = top[up, :] + sigma_ref[8 * s : 8 * s + 8, :]
    one = jnp.ones((8, 128), F32)
    sigma_ref[0:8, :] = one
    for p in range(2):
        reach[p, 0:8, :] = one
    zero = jnp.zeros((1, 128), F32)
    show_ref[0:1, :] = zero
    show_ref[S : S + 1, :] = zero
    fold_ref[0:1, :] = zero
    fold_ref[S : S + 1, :] = zero
    for s in range(1, S):
        up = at(parent_ref[s])
        sigma = sigma_ref[8 * s : 8 * s + 8, :] / top[up, :]
        sigma_ref[8 * s : 8 * s + 8, :] = sigma
        actor = (depth[s] + 1) & 1
        actor_ref[s] = actor
        for p in range(2):
            weight = jnp.where(actor == p, sigma, one)
            reach[p, 8 * s : 8 * s + 8, :] = weight * reach[p, up, :]
        leaf = 1 - inner[s]
        folds = jnp.where(action_ref[s] == 0, leaf, 0)
        shows = (leaf - folds).astype(F32)
        folds = folds.astype(F32)
        for p in range(2):
            show_ref[p * S + s : p * S + s + 1, :] = jnp.full((1, 128), shows, F32)
            sign = jnp.where(actor == p, -folds, folds)
            fold_ref[p * S + s : p * S + s + 1, :] = jnp.full((1, 128), sign, F32)
    for p in range(2):
        for r in range(8):
            reach_ref[p * S : p * S + S, 128 * r : 128 * r + 128] = reach[
                1 - p, pl.ds(r, S, stride=8), :
            ].astype(BF)


def pieces(width):
    return [(a, min(a + 256, width)) for a in range(0, width, 256)]


def board(row, reach_ref, show, fold, compat_ref, gather_ref, spread_ref, code_ref,
          sums, vcol, onehot, left, diag, terms):
    rank_row = coded(row >> 16)
    slot_row = coded(row & 65535).astype(BF)
    for j in range(HP // 128):
        lanes = slice(128 * j, 128 * j + 128)
        down = jnp.broadcast_to(rank_row[:, lanes], (8, 128)).T
        vcol[lanes, :] = jnp.broadcast_to(down[:, 0:1], (128, 128)).astype(BF)
        onehot[:, lanes] = jnp.where(
            slot_row[:, lanes] == code_ref[...], jnp.ones((), BF), jnp.zeros((), BF)
        )
    rank_row = rank_row.astype(BF)
    for a, b in pieces(HP):
        spread = jnp.dot(reach_ref[...], onehot[:, a:b], preferred_element_type=F32).astype(BF)
        for c in range(a, b, 128):
            part = spread[:, c - a : c - a + 128]
            left[:, c : c + 128] = part * show
            diag[:, c : c + 128] = part * fold
    cards = jnp.dot(diag[...], gather_ref[...], preferred_element_type=F32)
    high = cards.astype(BF).astype(F32)
    lane = lax.broadcasted_iota(jnp.int32, cards.shape, 1)
    left[:, HP:] = jnp.where(lane < 64, high, cards - high).astype(BF)
    for a, b in pieces(HP):
        limit = compat_ref[:, a:b]
        gap = rank_row[:, a:b] - jnp.concatenate([vcol[...]] * ((b - a) // 128), axis=1)
        against = jnp.minimum(jnp.maximum(gap, -limit), limit)
        right = jnp.concatenate([against, spread_ref[:, a:b]], axis=0)
        chosen = jnp.dot(left[...], right, preferred_element_type=F32)
        chosen = chosen + diag[:, a:b].astype(F32)
        count = lax.broadcasted_iota(jnp.int32, chosen.shape, 0) == 0
        chosen = jnp.where(count, 1.0, chosen)
        high = chosen.astype(BF)
        terms[0 : 2 * S, a:b] = high
        terms[2 * S :, a:b] = (chosen - high.astype(F32)).astype(BF)
    for a, b in pieces(WIN):
        got = lax.dot_general(
            terms[...], onehot[a:b, :], (((1,), (1,)), ((), ())), preferred_element_type=F32
        )
        sums[:, a:b] = sums[:, a:b] + got[: 2 * S] + got[2 * S :]


def board_kernel(
    there_ref, parent_ref, pot_ref, actor_ref, boards_any, reach_any, sigma_any,
    show_any, fold_any, compat_any, gather_any, spread_any, code_any, mine_ref, theirs_ref,
    boards, reach_ref, sigma_ref, compat_ref, gather_ref, spread_ref, code_ref,
    show_ref, fold_ref, sums, vcol, onehot, left, diag, terms, value, mine_list, sems,
):
    pairs = [(boards_any, boards), (code_any, code_ref), (reach_any, reach_ref), (gather_any, gather_ref),
             (spread_any, spread_ref), (compat_any, compat_ref), (sigma_any, sigma_ref),
             (show_any, show_ref), (fold_any, fold_ref)]
    copies = [pltpu.make_async_copy(a, b, sems.at[i]) for i, (a, b) in enumerate(pairs)]
    for copy in copies:
        copy.start()
    sums[...] = jnp.zeros(sums.shape, F32)
    seq, hand = lax.axis_index("seq"), lax.axis_index("hand")

    def enlist(i, kept):
        mine_list[kept] = i
        return kept + there_ref[i]

    kept = lax.fori_loop(0, there_ref.shape[0], enlist, jnp.int32(0))
    for copy in copies:
        copy.wait()
    show = show_ref[...].astype(BF)
    fold = fold_ref[...].astype(BF)

    def step(i, carry):
        index = mine_list[i]
        board(boards[index >> 2, pl.ds(index & 3, 1), :], reach_ref, show, fold, compat_ref, gather_ref,
              spread_ref, code_ref, sums, vcol, onehot, left, diag, terms)
        return carry

    lax.fori_loop(0, kept, step, 0)
    for p in range(2):
        for r in range(8):
            value[p, pl.ds(r, S, stride=8), :] = sums[p * S : p * S + S, 128 * r : 128 * r + 128]

    def at(s):
        return pl.ds(pl.multiple_of(8 * s, 8), 8)

    def put(place, tile):
        turned = jnp.concatenate([tile[4:], tile[:4]], axis=0)
        tile = jnp.where(hand == 0, tile, turned)
        mine_ref[place] = tile[:4]
        theirs_ref[place] = tile[4:]

    mass = value[0, 0:8, :]
    for k in range(4):
        put((k, pl.ds(192, 4)), mass)
    value[0, 0:8, :] = jnp.zeros((8, 128), F32)
    for s in range(1, S):
        scale = pot_ref[s].astype(F32) / H
        for p in range(2):
            value[p, 8 * s : 8 * s + 8, :] = value[p, 8 * s : 8 * s + 8, :] * scale
    for s in range(S - 1, 0, -1):
        up = at(parent_ref[s])
        sigma = sigma_ref[8 * s : 8 * s + 8, :]
        actor = actor_ref[s]
        for p in range(2):
            own = value[p, 8 * s : 8 * s + 8, :]
            value[p, up, :] = value[p, up, :] + jnp.where(actor == p, sigma, 1.0) * own
    for s in range(S):
        chunk = jnp.bitwise_xor(seq, s // 16)
        row = 4 * (s % 16)
        for p in range(2):
            put((chunk, pl.ds(64 * p + row, 4)), value[p, 8 * s : 8 * s + 8, :])
        if s == 0:
            put((chunk, pl.ds(128 + row, 4)), jnp.zeros((8, 128), F32))
        else:
            up = at(parent_ref[s])
            actor = actor_ref[s]
            own = jnp.where(actor == 0, value[0, 8 * s : 8 * s + 8, :], value[1, 8 * s : 8 * s + 8, :])
            over = jnp.where(actor == 0, value[0, up, :], value[1, up, :])
            put((chunk, pl.ds(128 + row, 4)), own - over)


def finish_kernel(logits_ref, mine, got, c1, c2, c3, new_ref, values_ref, total):
    total[...] = ((mine[0] + got[0]) + c1[...]) + (c2[...] + c3[...])
    for r in range(4):
        mass = total[192 + r : 193 + r, :] + 1.0
        lanes = slice(128 * r, 128 * r + 128)
        for p in range(2):
            values_ref[p, :, lanes] = total[pl.ds(64 * p + r, 16, stride=4), :] / mass
        gain = total[pl.ds(128 + r, 16, stride=4), :] / mass
        new_ref[:, lanes] = logits_ref[:, lanes] + STEP * gain


def swap(x, axis, size, bits):
    return lax.ppermute(x, axis, [(i, i ^ bits) for i in range(size)])


def local(board_cards, ranks, buckets, parent, action, pot, logits):
    sds = jax.ShapeDtypeStruct
    pair, compat, gather, spread, code = constants()
    groups, planes = lax.axis_size("boards"), 8
    boards = board_cards.shape[0]
    slots = boards // planes
    blocks = [swap(logits, "seq", 4, k) for k in range(1, 4)]
    own = pl.pallas_call(
        prep_kernel,
        compiler_params=pltpu.CompilerParams(vmem_limit_bytes=60 * 2**20),
        out_shape=sds((groups, slots, HP), jnp.int32),
        in_specs=[VM, VM, VM, VM],
        out_specs=VM,
        scratch_shapes=[pltpu.VMEM((boards, HQ), jnp.int32)],
    )(board_cards.T, ranks, buckets, jnp.asarray(pair))
    own, blocks = lax.optimization_barrier((own, blocks))
    packs = lax.all_to_all(own, "boards", 0, 0)
    blocks = [logits] + blocks
    blocks = blocks + [swap(x, "hand", 2, 1) for x in blocks]
    reach, sigma, show, fold, actor = pl.pallas_call(
        reach_kernel,
        compiler_params=pltpu.CompilerParams(vmem_limit_bytes=8 * 2**20),
        out_shape=[sds((2 * S, WIN), BF), sds((8 * S, 128), F32), sds((2 * S, 128), F32),
                   sds((2 * S, 128), F32), sds((S,), jnp.int32)],
        in_specs=[SM] * 2 + [VM] * 8,
        out_specs=[VM] * 4 + [SM],
        scratch_shapes=[
            pltpu.VMEM((8 * S, 128), F32),
            pltpu.VMEM((8 * S, 128), F32),
            pltpu.VMEM((2, 8 * S, 128), F32),
            pltpu.SMEM((S,), jnp.int32),
            pltpu.SMEM((S,), jnp.int32),
        ],
        cost_estimate=pl.CostEstimate(flops=4_000_000, bytes_accessed=2_000_000, transcendentals=65536),
    )(parent, action, *blocks)
    there = packs[:, :, LIVE].reshape(groups * slots) >> 16
    mine, theirs = pl.pallas_call(
        board_kernel,
        out_shape=[sds((4, 200, 128), F32)] * 2,
        in_specs=[SM] * 4 + [HB] * 9,
        out_specs=[VM] * 2,
        scratch_shapes=[
            pltpu.VMEM((groups, slots, HP), jnp.int32),
            pltpu.VMEM((2 * S, WIN), BF),
            pltpu.VMEM((8 * S, 128), F32),
            pltpu.VMEM((HP, HP), BF),
            pltpu.VMEM((HP, EXT), BF),
            pltpu.VMEM((EXT, HP), BF),
            pltpu.VMEM((WIN, 128), BF),
            pltpu.VMEM((2 * S, 128), F32),
            pltpu.VMEM((2 * S, 128), F32),
            pltpu.VMEM((2 * S, WIN), F32),
            pltpu.VMEM((HP, 128), BF),
            pltpu.VMEM((WIN, HP), BF),
            pltpu.VMEM((2 * S, HP + EXT), BF),
            pltpu.VMEM((2 * S, HP), BF),
            pltpu.VMEM((4 * S, HP), BF),
            pltpu.VMEM((2, 8 * S, 128), F32),
            pltpu.SMEM((groups * slots + 8,), jnp.int32),
            pltpu.SemaphoreType.DMA((9,)),
        ],
        compiler_params=pltpu.CompilerParams(vmem_limit_bytes=40 * 2**20),
        cost_estimate=pl.CostEstimate(flops=8_000_000_000, bytes_accessed=8_000_000, transcendentals=0),
    )(there, parent, pot, actor, packs, reach, sigma, show, fold,
      jnp.asarray(compat), jnp.asarray(gather), jnp.asarray(spread), jnp.asarray(code))
    got = swap(theirs, "hand", 2, 1)
    chunks = [swap(mine[k] + got[k], "seq", 4, k) for k in range(1, 4)]
    new_logits, values = pl.pallas_call(
        finish_kernel,
        compiler_params=pltpu.CompilerParams(vmem_limit_bytes=8 * 2**20),
        out_shape=[sds(logits.shape, F32), sds((2,) + logits.shape, F32)],
        in_specs=[VM] * 6,
        out_specs=[VM] * 2,
        scratch_shapes=[pltpu.VMEM((200, 128), F32)],
    )(logits, mine, got, *chunks)
    return new_logits, values


def solution(mesh):
    return jax.shard_map(
        local,
        mesh=mesh,
        in_specs=(
            P("boards", None),
            P("boards", None),
            P("boards", None),
            P(),
            P(),
            P(),
            P("seq", ("boards", "hand")),
        ),
        out_specs=(P("seq", ("boards", "hand")), P(None, "seq", ("boards", "hand"))),
        check_vma=False,
    )
```

```python
import functools

import jax
import jax.numpy as jnp
import ml_dtypes
import numpy as np
from jax import lax
from jax.experimental import pallas as pl
from jax.experimental.pallas import tpu as pltpu
from jax.sharding import PartitionSpec as P

CARDS = 52
FREE = CARDS - 5
S = 64
WIN = 1024
H = CARDS * (CARDS - 1) // 2
LIVE = FREE * (FREE - 1) // 2
HQ = 1408
HP = 1152
EXT = 128
DEAD = 2047
STEP = 0.5
BF = jnp.bfloat16
F32 = jnp.float32
VM = pl.BlockSpec(memory_space=pltpu.VMEM)
SM = pl.BlockSpec(memory_space=pltpu.SMEM)
AN = pl.BlockSpec(memory_space=pl.ANY)


def constants():
    pair = np.full((2, HQ), CARDS, np.int32)
    pair[:, :H] = np.triu_indices(CARDS, 1)
    first, second = np.triu_indices(FREE, 1)
    held = np.zeros((HP, 64), np.float32)
    held[np.arange(LIVE), first] = 1
    held[np.arange(LIVE), second] = 1
    compat = np.zeros((HP, HP), np.float32)
    compat[:LIVE, :LIVE] = (held @ held.T)[:LIVE, :LIVE] == 0
    held[:LIVE, FREE] = 1
    gather = np.concatenate([held, held], axis=1)
    held[:, :FREE] *= -1
    spread = np.concatenate([held, held], axis=1).T
    k = np.arange(WIN)
    code = np.broadcast_to(((128 + k % 128) * 2.0 ** (k // 128))[:, None], (WIN, 128))
    code = np.pad(code, ((0, HP - WIN), (0, 0)))
    fixed = np.concatenate([compat, gather, code], axis=1)
    fixed = np.concatenate([fixed, np.pad(spread, ((0, 0), (0, EXT + 128)))], axis=0)
    return pair, np.asarray(fixed, ml_dtypes.bfloat16)


def coded(value):
    power = jnp.ones(value.shape, F32)
    for bit in range(6):
        on = (value >> (7 + bit)) & 1
        power = power * jnp.where(on == 1, float(2 ** (2**bit)), 1.0)
    return ((value & 127) + 128).astype(F32) * power


def prep_kernel(cards_ref, ranks_ref, buckets_ref, pair_ref, out_ref, wide):
    boards = buckets_ref.shape[0]
    wide[:, 0:H] = ranks_ref[...] * 2048 + (buckets_ref[...] & (WIN - 1))
    lanes = lax.broadcasted_iota(jnp.int32, (1, HQ), 1)
    row = lax.broadcasted_iota(jnp.int32, (boards, boards), 0)
    col = lax.broadcasted_iota(jnp.int32, (boards, boards), 1)

    def across(key):
        return jnp.sum(jnp.where(row == col, key.astype(F32), 0.0), axis=0, keepdims=True)

    def down(key):
        return jnp.sum(jnp.where(row == col, key.astype(F32), 0.0), axis=1, keepdims=True).astype(jnp.int32)

    first, second = pair_ref[0:1, :], pair_ref[1:2, :]
    low, high = first, second
    dead = lanes >= H
    for c in range(5):
        card = down(cards_ref[c : c + 1, :])
        dead = dead | (first == card) | (second == card)
        low = low - jnp.where(card < first, 1, 0)
        high = high - jnp.where(card < second, 1, 0)
    shift = lanes - (((low * (2 * FREE - 1 - low)) >> 1) + high - low - 1)
    word = jnp.where(dead, DEAD, (wide[...] & 0xFFFFFF) + (shift << 24))
    for bit in range(8):
        moved = pltpu.roll(word, HQ - (1 << bit), 1)
        stays = ((word >> (24 + bit)) & 1) == 0
        word = jnp.where(((moved >> (24 + bit)) & 1) == 1, moved, jnp.where(stays, word, DEAD))
    word = jnp.where(lanes[:, :HP] < LIVE, word[:, :HP] & 0xFFFFFF, 2048 + DEAD)
    plane = 2 * lax.axis_index("seq") + lax.axis_index("hand")
    group = lax.axis_index("boards")
    cluster = buckets_ref[:, 0:1] // WIN
    twin = (across(cluster) == cluster.astype(F32)) & (col < row)
    twins = jnp.sum(jnp.where(twin, 1.0, 0.0), axis=1, keepdims=True).astype(jnp.int32)
    slots = out_ref.shape[1]
    slot = jnp.where(
        ((cluster + (group >> 1) + 4 * (group & 1) + twins) & 7) == plane, slots * cluster + (twins >> 3), -1
    )
    taken = lax.broadcasted_iota(jnp.int32, (slots * out_ref.shape[0], boards), 0).astype(F32) == across(slot)
    taken = jnp.where(taken, 1.0, 0.0).astype(BF)

    def deal(shift):
        part = ((word >> shift) & 255).astype(F32).astype(BF)
        return jnp.dot(taken, part, preferred_element_type=F32).astype(jnp.int32)

    word = deal(0) + (deal(8) << 8) + (deal(16) << 16)
    word = ((word >> 11) << 16) + (word & 2047)
    for c in range(out_ref.shape[0]):
        out_ref[c] = word[slots * c : slots * c + slots, :]


def tree_scalars(parent_ref, depth, inner):
    depth[0] = 0
    for s in range(S):
        inner[s] = 0
    for s in range(1, S):
        up = parent_ref[s]
        depth[s] = depth[up] + 1
        inner[up] = 1


def reach_kernel(parent_ref, action_ref, pot_ref, *refs):
    blocks = refs[:8]
    reach_ref, sigma_ref, show_ref, fold_ref, table_ref = refs[8:13]
    line, top, reach, depth, inner = refs[13:]
    seq, hand = lax.axis_index("seq"), lax.axis_index("hand")
    tree_scalars(parent_ref, depth, inner)
    table_ref[0] = 1
    table_ref[S] = 0
    table_ref[2 * S] = 0
    for k in range(4):
        base = 128 * jnp.bitwise_xor(seq, k)
        for half in range(2):
            start = base + 4 * jnp.bitwise_xor(hand, half)
            for r in range(4):
                line[pl.ds(start + r, 16, stride=8), :] = blocks[4 * half + k][
                    :, 128 * r : 128 * r + 128
                ]

    def at(s):
        return pl.ds(pl.multiple_of(8 * s, 8), 8)

    top[...] = jnp.full(top.shape, -jnp.inf, F32)
    for s in range(1, S):
        up = at(parent_ref[s])
        top[up, :] = jnp.maximum(top[up, :], line[8 * s : 8 * s + 8, :])
    for s in range(1, S):
        up = at(parent_ref[s])
        sigma_ref[8 * s : 8 * s + 8, :] = jnp.exp(line[8 * s : 8 * s + 8, :] - top[up, :])
    top[...] = jnp.zeros(top.shape, F32)
    for s in range(1, S):
        up = at(parent_ref[s])
        top[up, :] = top[up, :] + sigma_ref[8 * s : 8 * s + 8, :]
    one = jnp.ones((8, 128), F32)
    sigma_ref[0:8, :] = one
    for p in range(2):
        reach[p, 0:8, :] = one
    zero = jnp.zeros((1, 128), F32)
    show_ref[0:1, :] = zero
    show_ref[S : S + 1, :] = zero
    fold_ref[0:1, :] = zero
    fold_ref[S : S + 1, :] = zero
    for s in range(1, S):
        up = at(parent_ref[s])
        sigma = sigma_ref[8 * s : 8 * s + 8, :] / top[up, :]
        sigma_ref[8 * s : 8 * s + 8, :] = sigma
        actor = (depth[s] + 1) & 1
        table_ref[s] = actor
        table_ref[S + s] = parent_ref[s]
        table_ref[2 * S + s] = pot_ref[s]
        for p in range(2):
            weight = jnp.where(actor == p, sigma, one)
            reach[p, 8 * s : 8 * s + 8, :] = weight * reach[p, up, :]
        leaf = 1 - inner[s]
        folds = jnp.where(action_ref[s] == 0, leaf, 0)
        shows = (leaf - folds).astype(F32)
        folds = folds.astype(F32)
        for p in range(2):
            show_ref[p * S + s : p * S + s + 1, :] = jnp.full((1, 128), shows, F32)
            sign = jnp.where(actor == p, -folds, folds)
            fold_ref[p * S + s : p * S + s + 1, :] = jnp.full((1, 128), sign, F32)
    for p in range(2):
        for r in range(8):
            reach_ref[p * S : p * S + S, 128 * r : 128 * r + 128] = reach[
                1 - p, pl.ds(r, S, stride=8), :
            ].astype(BF)


def pieces(width):
    return [(a, min(a + 256, width)) for a in range(0, width, 256)]


def give(row, reach_ref, show, fold, gather_ref, code_ref, vcol, onehot, left, diag, ranks):
    rank_row = coded(row >> 16)
    ranks[...] = rank_row
    slot_row = coded(row & 65535).astype(BF)
    for a, b in pieces(HP):
        parts = []
        for c in range(a, b, 128):
            down = jnp.broadcast_to(rank_row[:, c : c + 128], (8, 128)).T
            vcol[c : c + 128, :] = jnp.broadcast_to(down[:, 0:1], (128, 128)).astype(BF)
            parts.append(
                jnp.where(slot_row[:, c : c + 128] == code_ref[...], jnp.ones((), BF), jnp.zeros((), BF))
            )
        part = jnp.concatenate(parts, axis=1)
        onehot[:, a:b] = part
        spread = jnp.dot(reach_ref[...], part, preferred_element_type=F32).astype(BF)
        for c in range(a, b, 128):
            part = spread[:, c - a : c - a + 128]
            left[:, c : c + 128] = part * show
            diag[:, c : c + 128] = part * fold
    cards = jnp.dot(diag[...], gather_ref[...], preferred_element_type=F32)
    high = cards.astype(BF).astype(F32)
    lane = lax.broadcasted_iota(jnp.int32, cards.shape, 1)
    left[:, HP:] = jnp.where(lane < 64, high, cards - high).astype(BF)


def settle(compat_ref, spread_ref, sums, vcol, onehot, left, diag, terms, ranks):
    rank_row = ranks[...].astype(BF)
    for a, b in pieces(HP):
        limit = compat_ref[:, a:b]
        gap = rank_row[:, a:b] - jnp.concatenate([vcol[...]] * ((b - a) // 128), axis=1)
        against = jnp.minimum(jnp.maximum(gap, -limit), limit)
        right = jnp.concatenate([against, spread_ref[:, a:b]], axis=0)
        chosen = jnp.dot(left[...], right, preferred_element_type=F32)
        chosen = chosen + diag[:, a:b].astype(F32)
        count = lax.broadcasted_iota(jnp.int32, chosen.shape, 0) == 0
        chosen = jnp.where(count, 1.0, chosen)
        high = chosen.astype(BF)
        terms[0 : 2 * S, a:b] = high
        terms[2 * S :, a:b] = (chosen - high.astype(F32)).astype(BF)
    for a, b in pieces(WIN):
        got = lax.dot_general(
            terms[...], onehot[a:b, :], (((1,), (1,)), ((), ())), preferred_element_type=F32
        )
        sums[:, a:b] = sums[:, a:b] + got[: 2 * S] + got[2 * S :]


def board_kernel(
    there_ref, table_ref, boards, reach_ref, sigma_ref, show_ref, fold_ref, fixed_any,
    mine_ref, theirs_ref, compat_ref, gather_ref, spread_ref, code_ref,
    sums, vcol, onehot, left, diag, terms, value, ranks, mine_list, sems,
):
    pairs = [(fixed_any.at[pl.ds(0, WIN), pl.ds(HP + EXT, 128)], code_ref),
             (fixed_any.at[pl.ds(0, HP), pl.ds(HP, EXT)], gather_ref),
             (fixed_any.at[pl.ds(HP, EXT), pl.ds(0, HP)], spread_ref),
             (fixed_any.at[pl.ds(0, HP), pl.ds(0, HP)], compat_ref)]
    copies = [pltpu.make_async_copy(a, b, sems.at[i]) for i, (a, b) in enumerate(pairs)]
    for copy in copies:
        copy.start()
    sums[...] = jnp.zeros(sums.shape, F32)
    seq, hand = lax.axis_index("seq"), lax.axis_index("hand")

    def enlist(i, kept):
        mine_list[kept] = i
        return kept + there_ref[i]

    kept = lax.fori_loop(0, there_ref.shape[0], enlist, jnp.int32(0))
    show = show_ref[...].astype(BF)
    fold = fold_ref[...].astype(BF)

    def deal(i):
        index = mine_list[i]
        give(boards[index >> 2, pl.ds(index & 3, 1), :], reach_ref, show, fold, gather_ref, code_ref,
             vcol, onehot, left, diag, ranks)

    for copy in copies[:2]:
        copy.wait()
    deal(0)
    for copy in copies[2:]:
        copy.wait()

    def add():
        settle(compat_ref, spread_ref, sums, vcol, onehot, left, diag, terms, ranks)

    @pl.when(kept > 0)
    def _():
        add()

    def step(i, carry):
        deal(i)
        add()
        return carry

    lax.fori_loop(1, kept, step, 0)
    for p in range(2):
        for r in range(8):
            value[p, pl.ds(r, S, stride=8), :] = sums[p * S : p * S + S, 128 * r : 128 * r + 128]

    def at(s):
        return pl.ds(pl.multiple_of(8 * s, 8), 8)

    def put(place, tile):
        turned = jnp.concatenate([tile[4:], tile[:4]], axis=0)
        tile = jnp.where(hand == 0, tile, turned)
        mine_ref[place] = tile[:4]
        theirs_ref[place] = tile[4:]

    mass = value[0, 0:8, :]
    for k in range(4):
        put((k, pl.ds(192, 4)), mass)
    value[0, 0:8, :] = jnp.zeros((8, 128), F32)
    for s in range(1, S):
        scale = table_ref[2 * S + s].astype(F32) / H
        for p in range(2):
            value[p, 8 * s : 8 * s + 8, :] = value[p, 8 * s : 8 * s + 8, :] * scale
    for s in range(S - 1, 0, -1):
        up = at(table_ref[S + s])
        sigma = sigma_ref[8 * s : 8 * s + 8, :]
        actor = table_ref[s]
        for p in range(2):
            own = value[p, 8 * s : 8 * s + 8, :]
            value[p, up, :] = value[p, up, :] + jnp.where(actor == p, sigma, 1.0) * own
    for s in range(S):
        chunk = jnp.bitwise_xor(seq, s // 16)
        row = 4 * (s % 16)
        for p in range(2):
            put((chunk, pl.ds(64 * p + row, 4)), value[p, 8 * s : 8 * s + 8, :])
        if s == 0:
            put((chunk, pl.ds(128 + row, 4)), jnp.zeros((8, 128), F32))
        else:
            up = at(table_ref[S + s])
            actor = table_ref[s]
            own = jnp.where(actor == 0, value[0, 8 * s : 8 * s + 8, :], value[1, 8 * s : 8 * s + 8, :])
            over = jnp.where(actor == 0, value[0, up, :], value[1, up, :])
            put((chunk, pl.ds(128 + row, 4)), own - over)


def finish_kernel(logits_ref, mine, got, c1, c2, c3, new_ref, values_ref, total):
    total[...] = ((mine[0] + got[0]) + c1[...]) + (c2[...] + c3[...])
    for r in range(4):
        mass = total[192 + r : 193 + r, :] + 1.0
        lanes = slice(128 * r, 128 * r + 128)
        for p in range(2):
            values_ref[p, :, lanes] = total[pl.ds(64 * p + r, 16, stride=4), :] / mass
        gain = total[pl.ds(128 + r, 16, stride=4), :] / mass
        new_ref[:, lanes] = logits_ref[:, lanes] + STEP * gain


def swap(x, axis, size, bits):
    return lax.ppermute(x, axis, [(i, i ^ bits) for i in range(size)])


def local(board_cards, ranks, buckets, parent, action, pot, logits):
    sds = jax.ShapeDtypeStruct
    pair, fixed = constants()
    groups, planes = lax.axis_size("boards"), 8
    boards = board_cards.shape[0]
    slots = boards // planes
    blocks = [swap(logits, "seq", 4, k) for k in range(1, 4)]
    own = pl.pallas_call(
        prep_kernel,
        compiler_params=pltpu.CompilerParams(vmem_limit_bytes=60 * 2**20),
        out_shape=sds((groups, slots, HP), jnp.int32),
        in_specs=[VM, VM, VM, VM],
        out_specs=VM,
        scratch_shapes=[pltpu.VMEM((boards, HQ), jnp.int32)],
    )(board_cards.T, ranks, buckets, jnp.asarray(pair))
    own, blocks = lax.optimization_barrier((own, blocks))
    packs = lax.all_to_all(own, "boards", 0, 0)
    blocks = [logits] + blocks
    blocks = blocks + [swap(x, "hand", 2, 1) for x in blocks]
    reach, sigma, show, fold, table = pl.pallas_call(
        reach_kernel,
        compiler_params=pltpu.CompilerParams(vmem_limit_bytes=8 * 2**20),
        out_shape=[sds((2 * S, WIN), BF), sds((8 * S, 128), F32), sds((2 * S, 128), F32),
                   sds((2 * S, 128), F32), sds((3 * S,), jnp.int32)],
        in_specs=[SM] * 3 + [VM] * 8,
        out_specs=[VM] * 4 + [SM],
        scratch_shapes=[
            pltpu.VMEM((8 * S, 128), F32),
            pltpu.VMEM((8 * S, 128), F32),
            pltpu.VMEM((2, 8 * S, 128), F32),
            pltpu.SMEM((S,), jnp.int32),
            pltpu.SMEM((S,), jnp.int32),
        ],
        cost_estimate=pl.CostEstimate(flops=4_000_000, bytes_accessed=2_000_000, transcendentals=65536),
    )(parent, action, pot, *blocks)
    there = packs[:, :, LIVE].reshape(groups * slots) >> 16
    mine, theirs = pl.pallas_call(
        board_kernel,
        out_shape=[sds((4, 200, 128), F32)] * 2,
        in_specs=[SM] * 2 + [VM] * 5 + [AN],
        out_specs=[VM] * 2,
        scratch_shapes=[
            pltpu.VMEM((HP, HP), BF),
            pltpu.VMEM((HP, EXT), BF),
            pltpu.VMEM((EXT, HP), BF),
            pltpu.VMEM((WIN, 128), BF),
            pltpu.VMEM((2 * S, WIN), F32),
            pltpu.VMEM((HP, 128), BF),
            pltpu.VMEM((WIN, HP), BF),
            pltpu.VMEM((2 * S, HP + EXT), BF),
            pltpu.VMEM((2 * S, HP), BF),
            pltpu.VMEM((4 * S, HP), BF),
            pltpu.VMEM((2, 8 * S, 128), F32),
            pltpu.VMEM((1, HP), F32),
            pltpu.SMEM((groups * slots + 8,), jnp.int32),
            pltpu.SemaphoreType.DMA((4,)),
        ],
        compiler_params=pltpu.CompilerParams(vmem_limit_bytes=50 * 2**20),
        cost_estimate=pl.CostEstimate(flops=8_000_000_000, bytes_accessed=8_000_000, transcendentals=0),
    )(there, table, packs, reach, sigma, show, fold, jnp.asarray(fixed))
    got = swap(theirs, "hand", 2, 1)
    chunks = [swap(mine[k] + got[k], "seq", 4, k) for k in range(1, 4)]
    new_logits, values = pl.pallas_call(
        finish_kernel,
        compiler_params=pltpu.CompilerParams(vmem_limit_bytes=8 * 2**20),
        out_shape=[sds(logits.shape, F32), sds((2,) + logits.shape, F32)],
        in_specs=[VM] * 6,
        out_specs=[VM] * 2,
        scratch_shapes=[pltpu.VMEM((200, 128), F32)],
    )(logits, mine, got, *chunks)
    return new_logits, values


def solution(mesh):
    return jax.shard_map(
        local,
        mesh=mesh,
        in_specs=(
            P("boards", None),
            P("boards", None),
            P("boards", None),
            P(),
            P(),
            P(),
            P("seq", ("boards", "hand")),
        ),
        out_specs=(P("seq", ("boards", "hand")), P(None, "seq", ("boards", "hand"))),
        check_vma=False,
    )
```

```python
import functools

import jax
import jax.numpy as jnp
import ml_dtypes
import numpy as np
from jax import lax
from jax.experimental import pallas as pl
from jax.experimental.pallas import tpu as pltpu
from jax.sharding import PartitionSpec as P

CARDS = 52
FREE = CARDS - 5
S = 64
WIN = 1024
H = CARDS * (CARDS - 1) // 2
LIVE = FREE * (FREE - 1) // 2
HQ = 1408
HP = 1152
EXT = 128
DEAD = 2047
STEP = 0.5
BF = jnp.bfloat16
F32 = jnp.float32
VM = pl.BlockSpec(memory_space=pltpu.VMEM)
SM = pl.BlockSpec(memory_space=pltpu.SMEM)
AN = pl.BlockSpec(memory_space=pl.ANY)


def constants():
    pair = np.full((2, HQ), CARDS, np.int32)
    pair[:, :H] = np.triu_indices(CARDS, 1)
    first, second = np.triu_indices(FREE, 1)
    held = np.zeros((HP, 64), np.float32)
    held[np.arange(LIVE), first] = 1
    held[np.arange(LIVE), second] = 1
    compat = np.zeros((HP, HP), np.float32)
    compat[:LIVE, :LIVE] = (held @ held.T)[:LIVE, :LIVE] == 0
    held[:LIVE, FREE] = 1
    gather = np.concatenate([held, held], axis=1)
    held[:, :FREE] *= -1
    spread = np.concatenate([held, held], axis=1).T
    k = np.arange(WIN)
    code = np.broadcast_to(((128 + k % 128) * 2.0 ** (k // 128))[:, None], (WIN, 128))
    code = np.pad(code, ((0, HP - WIN), (0, 0)))
    fixed = np.concatenate([compat, gather, code], axis=1)
    fixed = np.concatenate([fixed, np.pad(spread, ((0, 0), (0, EXT + 128)))], axis=0)
    return pair, np.asarray(fixed, ml_dtypes.bfloat16)


def coded(value):
    power = jnp.ones(value.shape, F32)
    for bit in range(6):
        on = (value >> (7 + bit)) & 1
        power = power * jnp.where(on == 1, float(2 ** (2**bit)), 1.0)
    return ((value & 127) + 128).astype(F32) * power


def prep_kernel(cards_ref, ranks_ref, buckets_ref, pair_ref, out_ref, wide):
    boards = buckets_ref.shape[0]
    wide[:, 0:H] = ranks_ref[...] * 2048 + (buckets_ref[...] & (WIN - 1))
    lanes = lax.broadcasted_iota(jnp.int32, (1, HQ), 1)
    row = lax.broadcasted_iota(jnp.int32, (boards, boards), 0)
    col = lax.broadcasted_iota(jnp.int32, (boards, boards), 1)

    def across(key):
        return jnp.sum(jnp.where(row == col, key.astype(F32), 0.0), axis=0, keepdims=True)

    def down(key):
        return jnp.sum(jnp.where(row == col, key.astype(F32), 0.0), axis=1, keepdims=True).astype(jnp.int32)

    first, second = pair_ref[0:1, :], pair_ref[1:2, :]
    low, high = first, second
    dead = lanes >= H
    for c in range(5):
        card = down(cards_ref[c : c + 1, :])
        dead = dead | (first == card) | (second == card)
        low = low - jnp.where(card < first, 1, 0)
        high = high - jnp.where(card < second, 1, 0)
    shift = lanes - (((low * (2 * FREE - 1 - low)) >> 1) + high - low - 1)
    word = jnp.where(dead, DEAD, (wide[...] & 0xFFFFFF) + (shift << 24))
    for bit in range(8):
        moved = pltpu.roll(word, HQ - (1 << bit), 1)
        mark = jnp.int32(-(2**31) if bit == 7 else 2 ** (24 + bit))
        word = jnp.where(moved & mark != 0, moved, jnp.where(word & mark != 0, DEAD, word))
    word = jnp.where(lanes[:, :HP] < LIVE, word[:, :HP] & 0xFFFFFF, 2048 + DEAD)
    plane = 2 * lax.axis_index("seq") + lax.axis_index("hand")
    group = lax.axis_index("boards")
    cluster = buckets_ref[:, 0:1] // WIN
    twin = (across(cluster) == cluster.astype(F32)) & (col < row)
    twins = jnp.sum(jnp.where(twin, 1.0, 0.0), axis=1, keepdims=True).astype(jnp.int32)
    slots = out_ref.shape[1]
    slot = jnp.where(
        ((cluster + (group >> 1) + 4 * (group & 1) + twins) & 7) == plane, slots * cluster + (twins >> 3), -1
    )
    taken = lax.broadcasted_iota(jnp.int32, (slots * out_ref.shape[0], boards), 0).astype(F32) == across(slot)
    taken = jnp.where(taken, 1.0, 0.0).astype(BF)

    def deal(shift):
        part = ((word >> shift) & 255).astype(F32).astype(BF)
        return jnp.dot(taken, part, preferred_element_type=F32).astype(jnp.int32)

    word = deal(0) + (deal(8) << 8) + (deal(16) << 16)
    word = ((word >> 11) << 16) + (word & 2047)
    for c in range(out_ref.shape[0]):
        out_ref[c] = word[slots * c : slots * c + slots, :]


def tree_scalars(parent_ref, depth, inner):
    depth[0] = 0
    for s in range(S):
        inner[s] = 0
    for s in range(1, S):
        up = parent_ref[s]
        depth[s] = depth[up] + 1
        inner[up] = 1


def reach_kernel(parent_ref, action_ref, pot_ref, *refs):
    blocks = refs[:4]
    reach_ref, sigma_ref, show_ref, fold_ref, table_ref = refs[4:9]
    line, parts, top, reach, depth, inner = refs[9], refs[10:14], refs[14], refs[15:17], refs[17], refs[18]
    seq, hand = lax.axis_index("seq"), lax.axis_index("hand")
    tree_scalars(parent_ref, depth, inner)
    table_ref[0] = 1
    table_ref[S] = 0
    table_ref[2 * S] = 0
    for k in range(4):
        base = 128 * jnp.bitwise_xor(seq, k)
        for half in range(2):
            start = base + 4 * jnp.bitwise_xor(hand, half)
            for r in range(4):
                line[pl.ds(start + r, 16, stride=8), :] = blocks[k][
                    half, :, 128 * r : 128 * r + 128
                ]

    def at(s):
        return pl.ds(pl.multiple_of(8 * s, 8), 8)

    for part in parts:
        part[...] = jnp.full(part.shape, -jnp.inf, F32)
    for s in range(1, S):
        part, up = parts[s % 4], at(parent_ref[s])
        part[up, :] = jnp.maximum(part[up, :], line[8 * s : 8 * s + 8, :])
    top[...] = jnp.maximum(
        jnp.maximum(parts[0][...], parts[1][...]), jnp.maximum(parts[2][...], parts[3][...])
    )
    for part in parts:
        part[...] = jnp.zeros(part.shape, F32)
    for s in range(1, S):
        part, up = parts[s % 4], at(parent_ref[s])
        raised = jnp.exp(line[8 * s : 8 * s + 8, :] - top[up, :])
        sigma_ref[8 * s : 8 * s + 8, :] = raised
        part[up, :] = part[up, :] + raised
    top[...] = (parts[0][...] + parts[1][...]) + (parts[2][...] + parts[3][...])
    one = jnp.ones((8, 128), F32)
    sigma_ref[0:8, :] = one
    for p in range(2):
        reach[p][0:8, :] = one
    zero = jnp.zeros((1, 128), F32)
    show_ref[0:1, :] = zero
    show_ref[S : S + 1, :] = zero
    fold_ref[0:1, :] = zero
    fold_ref[S : S + 1, :] = zero
    for s in range(1, S):
        up = at(parent_ref[s])
        sigma = sigma_ref[8 * s : 8 * s + 8, :] / top[up, :]
        sigma_ref[8 * s : 8 * s + 8, :] = sigma
        actor = (depth[s] + 1) & 1
        table_ref[s] = actor
        table_ref[S + s] = parent_ref[s]
        table_ref[2 * S + s] = pot_ref[s]
        for p in range(2):
            weight = jnp.where(actor == p, sigma, one)
            reach[p][8 * s : 8 * s + 8, :] = weight * reach[p][up, :]
        leaf = 1 - inner[s]
        folds = jnp.where(action_ref[s] == 0, leaf, 0)
        shows = (leaf - folds).astype(F32)
        folds = folds.astype(F32)
        for p in range(2):
            show_ref[p * S + s : p * S + s + 1, :] = jnp.full((1, 128), shows, F32)
            sign = jnp.where(actor == p, -folds, folds)
            fold_ref[p * S + s : p * S + s + 1, :] = jnp.full((1, 128), sign, F32)
    for p in range(2):
        for r in range(8):
            reach_ref[p * S : p * S + S, 128 * r : 128 * r + 128] = reach[1 - p][
                pl.ds(r, S, stride=8), :
            ].astype(BF)


def pieces(width):
    return [(a, min(a + 256, width)) for a in range(0, width, 256)]


def give(row, reach_ref, show, fold, gather_ref, code_ref, vcol, onehot, left, diag, ranks):
    rank_row = coded(row >> 16)
    ranks[...] = rank_row
    slot_row = coded(row & 65535).astype(BF)
    for a, b in pieces(HP):
        parts = []
        for c in range(a, b, 128):
            down = jnp.broadcast_to(rank_row[:, c : c + 128], (8, 128)).T
            vcol[c : c + 128, :] = jnp.broadcast_to(down[:, 0:1], (128, 128)).astype(BF)
            parts.append(
                jnp.where(slot_row[:, c : c + 128] == code_ref[...], jnp.ones((), BF), jnp.zeros((), BF))
            )
        part = jnp.concatenate(parts, axis=1)
        onehot[:, a:b] = part
        spread = jnp.dot(reach_ref[...], part, preferred_element_type=F32).astype(BF)
        for c in range(a, b, 128):
            part = spread[:, c - a : c - a + 128]
            left[:, c : c + 128] = part * show
            diag[:, c : c + 128] = part * fold
    cards = jnp.dot(diag[...], gather_ref[...], preferred_element_type=F32)
    high = cards.astype(BF).astype(F32)
    lane = lax.broadcasted_iota(jnp.int32, cards.shape, 1)
    left[:, HP:] = jnp.where(lane < 64, high, cards - high).astype(BF)


def settle(compat_ref, spread_ref, sums, vcol, onehot, left, diag, terms, ranks):
    rank_row = ranks[...].astype(BF)
    for a, b in pieces(HP):
        limit = compat_ref[:, a:b]
        gap = rank_row[:, a:b] - jnp.concatenate([vcol[...]] * ((b - a) // 128), axis=1)
        against = jnp.minimum(jnp.maximum(gap, -limit), limit)
        right = jnp.concatenate([against, spread_ref[:, a:b]], axis=0)
        chosen = jnp.dot(left[...], right, preferred_element_type=F32)
        chosen = chosen + diag[:, a:b].astype(F32)
        count = lax.broadcasted_iota(jnp.int32, chosen.shape, 0) == 0
        chosen = jnp.where(count, 1.0, chosen)
        high = chosen.astype(BF)
        terms[0 : 2 * S, a:b] = high
        terms[2 * S :, a:b] = (chosen - high.astype(F32)).astype(BF)
    for a, b in pieces(WIN):
        got = lax.dot_general(
            terms[...], onehot[a:b, :], (((1,), (1,)), ((), ())), preferred_element_type=F32
        )
        sums[:, a:b] = sums[:, a:b] + got[: 2 * S] + got[2 * S :]


def board_kernel(
    there_ref, table_ref, boards, reach_ref, sigma_ref, show_ref, fold_ref, fixed_any,
    mine_ref, theirs_ref, compat_ref, gather_ref, spread_ref, code_ref,
    sums, vcol, onehot, left, diag, terms, value0, value1, ranks, mine_list, sems,
):
    pairs = [(fixed_any.at[pl.ds(0, WIN), pl.ds(HP + EXT, 128)], code_ref),
             (fixed_any.at[pl.ds(0, HP), pl.ds(HP, EXT)], gather_ref),
             (fixed_any.at[pl.ds(HP, EXT), pl.ds(0, HP)], spread_ref)]
    for a, b in pieces(HP):
        pairs.append((fixed_any.at[pl.ds(0, HP), pl.ds(a, b - a)], compat_ref.at[:, pl.ds(a, b - a)]))
    copies = [pltpu.make_async_copy(a, b, sems.at[i]) for i, (a, b) in enumerate(pairs)]
    for copy in copies:
        copy.start()
    sums[...] = jnp.zeros(sums.shape, F32)
    seq, hand = lax.axis_index("seq"), lax.axis_index("hand")

    def enlist(i, kept):
        mine_list[kept] = i
        return kept + there_ref[i >> 2, i & 3]

    kept = lax.fori_loop(0, there_ref.shape[0] * 4, enlist, jnp.int32(0))
    show = show_ref[...].astype(BF)
    fold = fold_ref[...].astype(BF)

    def deal(i):
        index = mine_list[i]
        give(boards[index >> 2, pl.ds(index & 3, 1), :], reach_ref, show, fold, gather_ref, code_ref,
             vcol, onehot, left, diag, ranks)

    for copy in copies[:2]:
        copy.wait()
    deal(0)
    for copy in copies[2:]:
        copy.wait()

    def add():
        settle(compat_ref, spread_ref, sums, vcol, onehot, left, diag, terms, ranks)

    @pl.when(kept > 0)
    def _():
        add()

    def step(i, carry):
        deal(i)
        add()
        return carry

    lax.fori_loop(1, kept, step, 0)
    value = (value0, value1)
    for p in range(2):
        for r in range(8):
            value[p][pl.ds(r, S, stride=8), :] = sums[p * S : p * S + S, 128 * r : 128 * r + 128]

    def at(s):
        return pl.ds(pl.multiple_of(8 * s, 8), 8)

    def put(place, tile):
        turned = jnp.concatenate([tile[4:], tile[:4]], axis=0)
        tile = jnp.where(hand == 0, tile, turned)
        mine_ref[place] = tile[:4]
        theirs_ref[place] = tile[4:]

    mass = value[0][0:8, :]
    for k in range(4):
        put((k, pl.ds(192, 4)), mass)
    value[0][0:8, :] = jnp.zeros((8, 128), F32)
    for s in range(1, S):
        scale = table_ref[2 * S + s].astype(F32) / H
        for p in range(2):
            value[p][8 * s : 8 * s + 8, :] = value[p][8 * s : 8 * s + 8, :] * scale
    for s in range(S - 1, 0, -1):
        up = at(table_ref[S + s])
        sigma = sigma_ref[8 * s : 8 * s + 8, :]
        actor = table_ref[s]
        for p in range(2):
            own = value[p][8 * s : 8 * s + 8, :]
            value[p][up, :] = value[p][up, :] + jnp.where(actor == p, sigma, 1.0) * own
    for s in range(S):
        chunk = jnp.bitwise_xor(seq, s // 16)
        row = 4 * (s % 16)
        for p in range(2):
            put((chunk, pl.ds(64 * p + row, 4)), value[p][8 * s : 8 * s + 8, :])
        if s == 0:
            put((chunk, pl.ds(128 + row, 4)), jnp.zeros((8, 128), F32))
        else:
            up = at(table_ref[S + s])
            actor = table_ref[s]
            own = jnp.where(actor == 0, value[0][8 * s : 8 * s + 8, :], value[1][8 * s : 8 * s + 8, :])
            over = jnp.where(actor == 0, value[0][up, :], value[1][up, :])
            put((chunk, pl.ds(128 + row, 4)), own - over)


def finish_kernel(logits_ref, mine, got, c1, c2, c3, new_ref, values_ref, total):
    total[...] = ((mine[0] + got[0]) + c1[...]) + (c2[...] + c3[...])
    for r in range(4):
        mass = total[192 + r : 193 + r, :] + 1.0
        lanes = slice(128 * r, 128 * r + 128)
        for p in range(2):
            values_ref[p, :, lanes] = total[pl.ds(64 * p + r, 16, stride=4), :] / mass
        gain = total[pl.ds(128 + r, 16, stride=4), :] / mass
        new_ref[:, lanes] = logits_ref[:, lanes] + STEP * gain


def swap(x, axis, size, bits):
    return lax.ppermute(x, axis, [(i, i ^ bits) for i in range(size)])


def local(board_cards, ranks, buckets, parent, action, pot, logits):
    sds = jax.ShapeDtypeStruct
    pair, fixed = constants()
    groups, planes = lax.axis_size("boards"), 8
    boards = board_cards.shape[0]
    slots = boards // planes
    other = swap(logits, "hand", 2, 1)
    own = pl.pallas_call(
        prep_kernel,
        compiler_params=pltpu.CompilerParams(vmem_limit_bytes=60 * 2**20),
        out_shape=sds((groups, slots, HP), jnp.int32),
        in_specs=[VM, VM, VM, VM],
        out_specs=VM,
        cost_estimate=pl.CostEstimate(flops=4_000_000_000, bytes_accessed=2_000_000, transcendentals=0),
        scratch_shapes=[pltpu.VMEM((boards, HQ), jnp.int32)],
    )(board_cards.T, ranks, buckets, jnp.asarray(pair))
    own, other = lax.optimization_barrier((own, other))
    wide = jnp.stack([logits, other])
    packs = lax.all_to_all(own, "boards", 0, 0)
    blocks = [wide] + [swap(wide, "seq", 4, k) for k in range(1, 4)]
    reach, sigma, show, fold, table = pl.pallas_call(
        reach_kernel,
        compiler_params=pltpu.CompilerParams(vmem_limit_bytes=8 * 2**20),
        out_shape=[sds((2 * S, WIN), BF), sds((8 * S, 128), F32), sds((2 * S, 128), F32),
                   sds((2 * S, 128), F32), sds((3 * S,), jnp.int32)],
        in_specs=[SM] * 3 + [VM] * 4,
        out_specs=[VM] * 4 + [SM],
        scratch_shapes=[
            pltpu.VMEM((8 * S, 128), F32),
            *[pltpu.VMEM((4 * S, 128), F32)] * 5,
            *[pltpu.VMEM((8 * S, 128), F32)] * 2,
            pltpu.SMEM((S,), jnp.int32),
            pltpu.SMEM((S,), jnp.int32),
        ],
        cost_estimate=pl.CostEstimate(flops=4_000_000, bytes_accessed=2_000_000, transcendentals=65536),
    )(parent, action, pot, *blocks)
    there = packs[:, :, LIVE] >> 16
    mine, theirs = pl.pallas_call(
        board_kernel,
        out_shape=[sds((4, 200, 128), F32)] * 2,
        in_specs=[SM] * 2 + [VM] * 5 + [AN],
        out_specs=[VM] * 2,
        scratch_shapes=[
            pltpu.VMEM((HP, HP), BF),
            pltpu.VMEM((HP, EXT), BF),
            pltpu.VMEM((EXT, HP), BF),
            pltpu.VMEM((WIN, 128), BF),
            pltpu.VMEM((2 * S, WIN), F32),
            pltpu.VMEM((HP, 128), BF),
            pltpu.VMEM((WIN, HP), BF),
            pltpu.VMEM((2 * S, HP + EXT), BF),
            pltpu.VMEM((2 * S, HP), BF),
            pltpu.VMEM((4 * S, HP), BF),
            *[pltpu.VMEM((8 * S, 128), F32)] * 2,
            pltpu.VMEM((1, HP), F32),
            pltpu.SMEM((groups * slots + 8,), jnp.int32),
            pltpu.SemaphoreType.DMA((8,)),
        ],
        compiler_params=pltpu.CompilerParams(vmem_limit_bytes=50 * 2**20),
        cost_estimate=pl.CostEstimate(flops=8_000_000_000, bytes_accessed=8_000_000, transcendentals=0),
    )(there, table, packs, reach, sigma, show, fold, jnp.asarray(fixed))
    got = swap(theirs, "hand", 2, 1)
    chunks = [swap(mine[k] + got[k], "seq", 4, k) for k in range(1, 4)]
    new_logits, values = pl.pallas_call(
        finish_kernel,
        compiler_params=pltpu.CompilerParams(vmem_limit_bytes=8 * 2**20),
        out_shape=[sds(logits.shape, F32), sds((2,) + logits.shape, F32)],
        in_specs=[VM] * 6,
        out_specs=[VM] * 2,
        scratch_shapes=[pltpu.VMEM((200, 128), F32)],
    )(logits, mine, got, *chunks)
    return new_logits, values


def solution(mesh):
    return jax.shard_map(
        local,
        mesh=mesh,
        in_specs=(
            P("boards", None),
            P("boards", None),
            P("boards", None),
            P(),
            P(),
            P(),
            P("seq", ("boards", "hand")),
        ),
        out_specs=(P("seq", ("boards", "hand")), P(None, "seq", ("boards", "hand"))),
        check_vma=False,
    )
```

```python
import functools

import jax
import jax.numpy as jnp
import ml_dtypes
import numpy as np
from jax import lax
from jax.experimental import pallas as pl
from jax.experimental.pallas import tpu as pltpu
from jax.sharding import PartitionSpec as P

CARDS = 52
FREE = CARDS - 5
S = 64
WIN = 1024
H = CARDS * (CARDS - 1) // 2
LIVE = FREE * (FREE - 1) // 2
HQ = 1408
HP = 1152
EXT = 128
DEAD = 2047
STEP = 0.5
BF = jnp.bfloat16
F32 = jnp.float32
VM = pl.BlockSpec(memory_space=pltpu.VMEM)
SM = pl.BlockSpec(memory_space=pltpu.SMEM)
AN = pl.BlockSpec(memory_space=pl.ANY)


def constants():
    pair = np.full((2, HQ), CARDS, np.int32)
    pair[:, :H] = np.triu_indices(CARDS, 1)
    first, second = np.triu_indices(FREE, 1)
    held = np.zeros((HP, 64), np.float32)
    held[np.arange(LIVE), first] = 1
    held[np.arange(LIVE), second] = 1
    compat = np.zeros((HP, HP), np.float32)
    compat[:LIVE, :LIVE] = (held @ held.T)[:LIVE, :LIVE] == 0
    held[:LIVE, FREE] = 1
    gather = np.concatenate([held, held], axis=1)
    held[:, :FREE] *= -1
    spread = np.concatenate([held, held], axis=1).T
    k = np.arange(WIN)
    code = np.broadcast_to(((128 + k % 128) * 2.0 ** (k // 128))[:, None], (WIN, 128))
    code = np.pad(code, ((0, HP - WIN), (0, 0)))
    fixed = np.concatenate([compat, gather, code], axis=1)
    fixed = np.concatenate([fixed, np.pad(spread, ((0, 0), (0, EXT + 128)))], axis=0)
    return pair, np.asarray(fixed, ml_dtypes.bfloat16)


def coded(value):
    power = jnp.ones(value.shape, F32)
    for bit in range(6):
        on = (value >> (7 + bit)) & 1
        power = power * jnp.where(on == 1, float(2 ** (2**bit)), 1.0)
    return ((value & 127) + 128).astype(F32) * power


def prep_kernel(cards_ref, ranks_ref, buckets_ref, pair_ref, out_ref, wide):
    boards = buckets_ref.shape[0]
    wide[:, 0:H] = ranks_ref[...] * 2048 + (buckets_ref[...] & (WIN - 1))
    lanes = lax.broadcasted_iota(jnp.int32, (1, HQ), 1)
    row = lax.broadcasted_iota(jnp.int32, (boards, boards), 0)
    col = lax.broadcasted_iota(jnp.int32, (boards, boards), 1)

    def across(key):
        return jnp.sum(jnp.where(row == col, key.astype(F32), 0.0), axis=0, keepdims=True)

    def down(key):
        return jnp.sum(jnp.where(row == col, key.astype(F32), 0.0), axis=1, keepdims=True).astype(jnp.int32)

    first, second = pair_ref[0:1, :], pair_ref[1:2, :]
    low, high = first, second
    dead = lanes >= H
    for c in range(5):
        card = down(cards_ref[c : c + 1, :])
        dead = dead | (first == card) | (second == card)
        low = low - jnp.where(card < first, 1, 0)
        high = high - jnp.where(card < second, 1, 0)
    shift = lanes - (((low * (2 * FREE - 1 - low)) >> 1) + high - low - 1)
    word = jnp.where(dead, DEAD, (wide[...] & 0xFFFFFF) + (shift << 24))
    for bit in range(8):
        moved = pltpu.roll(word, HQ - (1 << bit), 1)
        mark = jnp.int32(-(2**31) if bit == 7 else 2 ** (24 + bit))
        word = jnp.where(moved & mark != 0, moved, jnp.where(word & mark != 0, DEAD, word))
    seq, hand = lax.axis_index("seq"), lax.axis_index("hand")
    group = lax.axis_index("boards")
    cluster = buckets_ref[:, 0:1] // WIN
    same = across(cluster) == cluster.astype(F32)

    def count(mask):
        return jnp.sum(jnp.where(mask, 1.0, 0.0), axis=1, keepdims=True).astype(jnp.int32)

    twins = count(same & (col < row))
    few = count(same) <= 16
    turn = cluster + (group >> 1) + twins
    ours = jnp.where(few, turn & 3, turn & 7) == jnp.where(few, seq, seq + 4 * hand)
    slots = out_ref.shape[1]
    slot = jnp.where(ours, slots * cluster + jnp.where(few, twins >> 2, twins >> 3), -1)
    flag = jnp.where(few, 1, 2)
    word = jnp.where(lanes[:, :HP] < LIVE, word[:, :HP] & 0xFFFFFF, 2048 * flag + DEAD)
    taken = lax.broadcasted_iota(jnp.int32, (slots * out_ref.shape[0], boards), 0).astype(F32) == across(slot)
    taken = jnp.where(taken, 1.0, 0.0).astype(BF)

    def deal(shift):
        part = ((word >> shift) & 255).astype(F32).astype(BF)
        return jnp.dot(taken, part, preferred_element_type=F32).astype(jnp.int32)

    word = deal(0) + (deal(8) << 8) + (deal(16) << 16)
    word = ((word >> 11) << 16) + (word & 2047)
    for c in range(out_ref.shape[0]):
        out_ref[c] = word[slots * c : slots * c + slots, :]


def tree_scalars(parent_ref, depth, inner):
    depth[0] = 0
    for s in range(S):
        inner[s] = 0
    for s in range(1, S):
        up = parent_ref[s]
        depth[s] = depth[up] + 1
        inner[up] = 1


def reach_kernel(parent_ref, action_ref, pot_ref, *refs):
    blocks = refs[:4]
    reach_ref, sigma_ref, show_ref, fold_ref, table_ref = refs[4:9]
    line, parts, top, reach, depth, inner = refs[9], refs[10:14], refs[14], refs[15:17], refs[17], refs[18]
    seq, hand = lax.axis_index("seq"), lax.axis_index("hand")
    tree_scalars(parent_ref, depth, inner)
    table_ref[0] = 1
    table_ref[S] = 0
    table_ref[2 * S] = 0
    for k in range(4):
        base = 128 * jnp.bitwise_xor(seq, k)
        for half in range(2):
            start = base + 4 * jnp.bitwise_xor(hand, half)
            for r in range(4):
                line[pl.ds(start + r, 16, stride=8), :] = blocks[k][
                    half, :, 128 * r : 128 * r + 128
                ]

    def at(s):
        return pl.ds(pl.multiple_of(8 * s, 8), 8)

    for part in parts:
        part[...] = jnp.full(part.shape, -jnp.inf, F32)
    for s in range(1, S):
        part, up = parts[s % 4], at(parent_ref[s])
        part[up, :] = jnp.maximum(part[up, :], line[8 * s : 8 * s + 8, :])
    top[...] = jnp.maximum(
        jnp.maximum(parts[0][...], parts[1][...]), jnp.maximum(parts[2][...], parts[3][...])
    )
    for part in parts:
        part[...] = jnp.zeros(part.shape, F32)
    for s in range(1, S):
        part, up = parts[s % 4], at(parent_ref[s])
        raised = jnp.exp(line[8 * s : 8 * s + 8, :] - top[up, :])
        sigma_ref[8 * s : 8 * s + 8, :] = raised
        part[up, :] = part[up, :] + raised
    top[...] = (parts[0][...] + parts[1][...]) + (parts[2][...] + parts[3][...])
    one = jnp.ones((8, 128), F32)
    sigma_ref[0:8, :] = one
    for p in range(2):
        reach[p][0:8, :] = one
    zero = jnp.zeros((1, 128), F32)
    show_ref[0:1, :] = zero
    show_ref[S : S + 1, :] = zero
    fold_ref[0:1, :] = zero
    fold_ref[S : S + 1, :] = zero
    for s in range(1, S):
        up = at(parent_ref[s])
        sigma = sigma_ref[8 * s : 8 * s + 8, :] / top[up, :]
        sigma_ref[8 * s : 8 * s + 8, :] = sigma
        actor = (depth[s] + 1) & 1
        table_ref[s] = actor
        table_ref[S + s] = parent_ref[s]
        table_ref[2 * S + s] = pot_ref[s]
        for p in range(2):
            weight = jnp.where(actor == p, sigma, one)
            reach[p][8 * s : 8 * s + 8, :] = weight * reach[p][up, :]
        leaf = 1 - inner[s]
        folds = jnp.where(action_ref[s] == 0, leaf, 0)
        shows = (leaf - folds).astype(F32)
        folds = folds.astype(F32)
        for p in range(2):
            show_ref[p * S + s : p * S + s + 1, :] = jnp.full((1, 128), shows, F32)
            sign = jnp.where(actor == p, -folds, folds)
            fold_ref[p * S + s : p * S + s + 1, :] = jnp.full((1, 128), sign, F32)
    for p in range(2):
        for r in range(8):
            reach_ref[p * S : p * S + S, 128 * r : 128 * r + 128] = reach[1 - p][
                pl.ds(r, S, stride=8), :
            ].astype(BF)


def pieces(width):
    return [(a, min(a + 256, width)) for a in range(0, width, 256)]


def give(row, reach_ref, show, fold, gather_ref, code_ref, vcol, onehot, left, diag, ranks):
    rank_row = coded(row >> 16)
    ranks[...] = rank_row
    slot_row = coded(row & 65535).astype(BF)
    for a, b in pieces(HP):
        parts = []
        for c in range(a, b, 128):
            down = jnp.broadcast_to(rank_row[:, c : c + 128], (8, 128)).T
            vcol[c : c + 128, :] = jnp.broadcast_to(down[:, 0:1], (128, 128)).astype(BF)
            parts.append(
                jnp.where(slot_row[:, c : c + 128] == code_ref[...], jnp.ones((), BF), jnp.zeros((), BF))
            )
        part = jnp.concatenate(parts, axis=1)
        onehot[:, a:b] = part
        spread = jnp.dot(reach_ref[...], part, preferred_element_type=F32).astype(BF)
        for c in range(a, b, 128):
            part = spread[:, c - a : c - a + 128]
            left[:, c : c + 128] = part * show
            diag[:, c : c + 128] = part * fold
    cards = jnp.dot(diag[...], gather_ref[...], preferred_element_type=F32)
    high = cards.astype(BF).astype(F32)
    lane = lax.broadcasted_iota(jnp.int32, cards.shape, 1)
    left[:, HP:] = jnp.where(lane < 64, high, cards - high).astype(BF)


def settle(compat_ref, spread_ref, sums, vcol, onehot, left, diag, terms, ranks):
    rank_row = ranks[...].astype(BF)
    for a, b in pieces(HP):
        limit = compat_ref[:, a:b]
        gap = rank_row[:, a:b] - jnp.concatenate([vcol[...]] * ((b - a) // 128), axis=1)
        against = jnp.minimum(jnp.maximum(gap, -limit), limit)
        right = jnp.concatenate([against, spread_ref[:, a:b]], axis=0)
        chosen = jnp.dot(left[...], right, preferred_element_type=F32)
        chosen = chosen + diag[:, a:b].astype(F32)
        count = lax.broadcasted_iota(jnp.int32, chosen.shape, 0) == 0
        chosen = jnp.where(count, 1.0, chosen)
        high = chosen.astype(BF)
        terms[0 : 2 * S, a:b] = high
        terms[2 * S :, a:b] = (chosen - high.astype(F32)).astype(BF)
    for a, b in pieces(WIN):
        got = lax.dot_general(
            terms[...], onehot[a:b, :], (((1,), (1,)), ((), ())), preferred_element_type=F32
        )
        sums[:, a:b] = sums[:, a:b] + got[: 2 * S] + got[2 * S :]


def board_kernel(
    there_ref, table_ref, boards, reach_ref, sigma_ref, show_ref, fold_ref, fixed_any,
    mine_ref, theirs_ref, compat_ref, gather_ref, spread_ref, code_ref,
    sums, vcol, onehot, left, diag, terms, value0, value1, ranks, mine_list, sems,
):
    pairs = [(fixed_any.at[pl.ds(0, WIN), pl.ds(HP + EXT, 128)], code_ref),
             (fixed_any.at[pl.ds(0, HP), pl.ds(HP, EXT)], gather_ref),
             (fixed_any.at[pl.ds(HP, EXT), pl.ds(0, HP)], spread_ref)]
    for a, b in pieces(HP):
        pairs.append((fixed_any.at[pl.ds(0, HP), pl.ds(a, b - a)], compat_ref.at[:, pl.ds(a, b - a)]))
    copies = [pltpu.make_async_copy(a, b, sems.at[i]) for i, (a, b) in enumerate(pairs)]
    for copy in copies:
        copy.start()
    sums[...] = jnp.zeros(sums.shape, F32)
    seq, hand = lax.axis_index("seq"), lax.axis_index("hand")

    kept, seen = jnp.int32(0), hand
    for i in range(4 * there_ref.shape[0]):
        flag = there_ref[i // 4, i % 4]
        both = flag & 1
        mine_list[kept] = i
        kept = kept + (flag >> 1) + (both & (1 - (seen & 1)))
        seen = seen + both

    show = show_ref[...].astype(BF)
    fold = fold_ref[...].astype(BF)

    def deal(i):
        index = mine_list[i]
        give(boards[index >> 2, pl.ds(index & 3, 1), :], reach_ref, show, fold, gather_ref, code_ref,
             vcol, onehot, left, diag, ranks)

    for copy in copies[:2]:
        copy.wait()
    deal(0)
    for copy in copies[2:]:
        copy.wait()

    def add():
        settle(compat_ref, spread_ref, sums, vcol, onehot, left, diag, terms, ranks)

    @pl.when(kept > 0)
    def _():
        add()

    def step(i, carry):
        deal(i)
        add()
        return carry

    lax.fori_loop(1, kept, step, 0)
    value = (value0, value1)
    for p in range(2):
        for r in range(8):
            value[p][pl.ds(r, S, stride=8), :] = sums[p * S : p * S + S, 128 * r : 128 * r + 128]

    def at(s):
        return pl.ds(pl.multiple_of(8 * s, 8), 8)

    def put(place, tile):
        turned = jnp.concatenate([tile[4:], tile[:4]], axis=0)
        tile = jnp.where(hand == 0, tile, turned)
        mine_ref[place] = tile[:4]
        theirs_ref[place] = tile[4:]

    mass = value[0][0:8, :]
    for k in range(4):
        put((k, pl.ds(192, 4)), mass)
    value[0][0:8, :] = jnp.zeros((8, 128), F32)
    for s in range(1, S):
        scale = table_ref[2 * S + s].astype(F32) / H
        for p in range(2):
            value[p][8 * s : 8 * s + 8, :] = value[p][8 * s : 8 * s + 8, :] * scale
    for s in range(S - 1, 0, -1):
        up = at(table_ref[S + s])
        sigma = sigma_ref[8 * s : 8 * s + 8, :]
        actor = table_ref[s]
        for p in range(2):
            own = value[p][8 * s : 8 * s + 8, :]
            value[p][up, :] = value[p][up, :] + jnp.where(actor == p, sigma, 1.0) * own
    for s in range(S):
        chunk = jnp.bitwise_xor(seq, s // 16)
        row = 4 * (s % 16)
        for p in range(2):
            put((chunk, pl.ds(64 * p + row, 4)), value[p][8 * s : 8 * s + 8, :])
        if s == 0:
            put((chunk, pl.ds(128 + row, 4)), jnp.zeros((8, 128), F32))
        else:
            up = at(table_ref[S + s])
            actor = table_ref[s]
            own = jnp.where(actor == 0, value[0][8 * s : 8 * s + 8, :], value[1][8 * s : 8 * s + 8, :])
            over = jnp.where(actor == 0, value[0][up, :], value[1][up, :])
            put((chunk, pl.ds(128 + row, 4)), own - over)


def finish_kernel(logits_ref, mine, got, c1, c2, c3, new_ref, values_ref, total):
    total[...] = ((mine[0] + got[0]) + c1[...]) + (c2[...] + c3[...])
    for r in range(4):
        mass = total[192 + r : 193 + r, :] + 1.0
        lanes = slice(128 * r, 128 * r + 128)
        for p in range(2):
            values_ref[p, :, lanes] = total[pl.ds(64 * p + r, 16, stride=4), :] / mass
        gain = total[pl.ds(128 + r, 16, stride=4), :] / mass
        new_ref[:, lanes] = logits_ref[:, lanes] + STEP * gain


def swap(x, axis, size, bits):
    return lax.ppermute(x, axis, [(i, i ^ bits) for i in range(size)])


def local(board_cards, ranks, buckets, parent, action, pot, logits):
    sds = jax.ShapeDtypeStruct
    pair, fixed = constants()
    groups, planes = lax.axis_size("boards"), 8
    boards = board_cards.shape[0]
    slots = boards // planes
    other = swap(logits, "hand", 2, 1)
    own = pl.pallas_call(
        prep_kernel,
        compiler_params=pltpu.CompilerParams(vmem_limit_bytes=60 * 2**20),
        out_shape=sds((groups, slots, HP), jnp.int32),
        in_specs=[VM, VM, VM, VM],
        out_specs=VM,
        cost_estimate=pl.CostEstimate(flops=4_000_000_000, bytes_accessed=2_000_000, transcendentals=0),
        scratch_shapes=[pltpu.VMEM((boards, HQ), jnp.int32)],
    )(board_cards.T, ranks, buckets, jnp.asarray(pair))
    own, other = lax.optimization_barrier((own, other))
    wide = jnp.stack([logits, other])
    packs = lax.all_to_all(own, "boards", 0, 0)
    blocks = [wide] + [swap(wide, "seq", 4, k) for k in range(1, 4)]
    reach, sigma, show, fold, table = pl.pallas_call(
        reach_kernel,
        compiler_params=pltpu.CompilerParams(vmem_limit_bytes=8 * 2**20),
        out_shape=[sds((2 * S, WIN), BF), sds((8 * S, 128), F32), sds((2 * S, 128), F32),
                   sds((2 * S, 128), F32), sds((3 * S,), jnp.int32)],
        in_specs=[SM] * 3 + [VM] * 4,
        out_specs=[VM] * 4 + [SM],
        scratch_shapes=[
            pltpu.VMEM((8 * S, 128), F32),
            *[pltpu.VMEM((4 * S, 128), F32)] * 5,
            *[pltpu.VMEM((8 * S, 128), F32)] * 2,
            pltpu.SMEM((S,), jnp.int32),
            pltpu.SMEM((S,), jnp.int32),
        ],
        cost_estimate=pl.CostEstimate(flops=4_000_000, bytes_accessed=2_000_000, transcendentals=65536),
    )(parent, action, pot, *blocks)
    there = packs[:, :, LIVE] >> 16
    mine, theirs = pl.pallas_call(
        board_kernel,
        out_shape=[sds((4, 200, 128), F32)] * 2,
        in_specs=[SM] * 2 + [VM] * 5 + [AN],
        out_specs=[VM] * 2,
        scratch_shapes=[
            pltpu.VMEM((HP, HP), BF),
            pltpu.VMEM((HP, EXT), BF),
            pltpu.VMEM((EXT, HP), BF),
            pltpu.VMEM((WIN, 128), BF),
            pltpu.VMEM((2 * S, WIN), F32),
            pltpu.VMEM((HP, 128), BF),
            pltpu.VMEM((WIN, HP), BF),
            pltpu.VMEM((2 * S, HP + EXT), BF),
            pltpu.VMEM((2 * S, HP), BF),
            pltpu.VMEM((4 * S, HP), BF),
            *[pltpu.VMEM((8 * S, 128), F32)] * 2,
            pltpu.VMEM((1, HP), F32),
            pltpu.SMEM((groups * slots + 8,), jnp.int32),
            pltpu.SemaphoreType.DMA((8,)),
        ],
        compiler_params=pltpu.CompilerParams(vmem_limit_bytes=50 * 2**20),
        cost_estimate=pl.CostEstimate(flops=8_000_000_000, bytes_accessed=8_000_000, transcendentals=0),
    )(there, table, packs, reach, sigma, show, fold, jnp.asarray(fixed))
    got = swap(theirs, "hand", 2, 1)
    chunks = [swap(mine[k] + got[k], "seq", 4, k) for k in range(1, 4)]
    new_logits, values = pl.pallas_call(
        finish_kernel,
        compiler_params=pltpu.CompilerParams(vmem_limit_bytes=8 * 2**20),
        out_shape=[sds(logits.shape, F32), sds((2,) + logits.shape, F32)],
        in_specs=[VM] * 6,
        out_specs=[VM] * 2,
        scratch_shapes=[pltpu.VMEM((200, 128), F32)],
    )(logits, mine, got, *chunks)
    return new_logits, values


def solution(mesh):
    return jax.shard_map(
        local,
        mesh=mesh,
        in_specs=(
            P("boards", None),
            P("boards", None),
            P("boards", None),
            P(),
            P(),
            P(),
            P("seq", ("boards", "hand")),
        ),
        out_specs=(P("seq", ("boards", "hand")), P(None, "seq", ("boards", "hand"))),
        check_vma=False,
    )
```

```python
import functools

import jax
import jax.numpy as jnp
import ml_dtypes
import numpy as np
from jax import lax
from jax.experimental import pallas as pl
from jax.experimental.pallas import tpu as pltpu
from jax.sharding import PartitionSpec as P

CARDS = 52
FREE = CARDS - 5
S = 64
WIN = 1024
H = CARDS * (CARDS - 1) // 2
LIVE = FREE * (FREE - 1) // 2
HQ = 1408
HP = 1152
EXT = 128
DEAD = 2047
STEP = 0.5
FAR_LAST = (1, 3, 2)
BF = jnp.bfloat16
F32 = jnp.float32
VM = pl.BlockSpec(memory_space=pltpu.VMEM)
SM = pl.BlockSpec(memory_space=pltpu.SMEM)
AN = pl.BlockSpec(memory_space=pl.ANY)


def constants():
    pair = np.full((2, HQ), CARDS, np.int32)
    pair[:, :H] = np.triu_indices(CARDS, 1)
    first, second = np.triu_indices(FREE, 1)
    held = np.zeros((HP, 64), np.float32)
    held[np.arange(LIVE), first] = 1
    held[np.arange(LIVE), second] = 1
    compat = np.zeros((HP, HP), np.float32)
    compat[:LIVE, :LIVE] = (held @ held.T)[:LIVE, :LIVE] == 0
    held[:LIVE, FREE] = 1
    gather = np.concatenate([held, held], axis=1)
    held[:, :FREE] *= -1
    spread = np.concatenate([held, held], axis=1).T
    k = np.arange(WIN)
    code = np.broadcast_to(((128 + k % 128) * 2.0 ** (k // 128))[:, None], (WIN, 128))
    code = np.pad(code, ((0, HP - WIN), (0, 0)))
    fixed = np.concatenate([compat, gather, code], axis=1)
    fixed = np.concatenate([fixed, np.pad(spread, ((0, 0), (0, EXT + 128)))], axis=0)
    return pair, np.asarray(fixed, ml_dtypes.bfloat16)


def coded(value):
    power = jnp.ones(value.shape, F32)
    for bit in range(6):
        on = (value >> (7 + bit)) & 1
        power = power * jnp.where(on == 1, float(2 ** (2**bit)), 1.0)
    return ((value & 127) + 128).astype(F32) * power


def prep_kernel(cards_ref, ranks_ref, buckets_ref, pair_ref, out_ref, wide):
    boards = buckets_ref.shape[0]
    wide[:, 0:H] = ranks_ref[...] * 2048 + (buckets_ref[...] & (WIN - 1))
    lanes = lax.broadcasted_iota(jnp.int32, (1, HQ), 1)
    row = lax.broadcasted_iota(jnp.int32, (boards, boards), 0)
    col = lax.broadcasted_iota(jnp.int32, (boards, boards), 1)

    def across(key):
        return jnp.sum(jnp.where(row == col, key.astype(F32), 0.0), axis=0, keepdims=True)

    def down(key):
        return jnp.sum(jnp.where(row == col, key.astype(F32), 0.0), axis=1, keepdims=True).astype(jnp.int32)

    first, second = pair_ref[0:1, :], pair_ref[1:2, :]
    low, high = first, second
    dead = lanes >= H
    for c in range(5):
        card = down(cards_ref[c : c + 1, :])
        dead = dead | (first == card) | (second == card)
        low = low - jnp.where(card < first, 1, 0)
        high = high - jnp.where(card < second, 1, 0)
    shift = lanes - (((low * (2 * FREE - 1 - low)) >> 1) + high - low - 1)
    word = jnp.where(dead, DEAD, (wide[...] & 0xFFFFFF) + (shift << 24))
    for bit in range(8):
        moved = pltpu.roll(word, HQ - (1 << bit), 1)
        mark = jnp.int32(-(2**31) if bit == 7 else 2 ** (24 + bit))
        word = jnp.where(moved & mark != 0, moved, jnp.where(word & mark != 0, DEAD, word))
    seq, hand = lax.axis_index("seq"), lax.axis_index("hand")
    group = lax.axis_index("boards")
    cluster = buckets_ref[:, 0:1] // WIN
    same = across(cluster) == cluster.astype(F32)

    def count(mask):
        return jnp.sum(jnp.where(mask, 1.0, 0.0), axis=1, keepdims=True).astype(jnp.int32)

    twins = count(same & (col < row))
    few = count(same) <= 16
    turn = cluster + (group >> 1) + twins
    ours = jnp.where(few, turn & 3, turn & 7) == jnp.where(few, seq, seq + 4 * hand)
    slots = out_ref.shape[1]
    slot = jnp.where(ours, slots * cluster + jnp.where(few, twins >> 2, twins >> 3), -1)
    flag = jnp.where(few, 1, 2)
    word = jnp.where(lanes[:, :HP] < LIVE, word[:, :HP] & 0xFFFFFF, 2048 * flag + DEAD)
    taken = lax.broadcasted_iota(jnp.int32, (slots * out_ref.shape[0], boards), 0).astype(F32) == across(slot)
    taken = jnp.where(taken, 1.0, 0.0).astype(BF)

    def deal(shift):
        part = ((word >> shift) & 255).astype(F32).astype(BF)
        return jnp.dot(taken, part, preferred_element_type=F32).astype(jnp.int32)

    word = deal(0) + (deal(8) << 8) + (deal(16) << 16)
    word = ((word >> 11) << 16) + (word & 2047)
    for c in range(out_ref.shape[0]):
        out_ref[c] = word[slots * c : slots * c + slots, :]


def tree_scalars(parent_ref, depth, inner):
    depth[0] = 0
    for s in range(S):
        inner[s] = 0
    for s in range(1, S):
        up = parent_ref[s]
        depth[s] = depth[up] + 1
        inner[up] = 1


def reach_kernel(parent_ref, action_ref, pot_ref, *refs):
    blocks = refs[:4]
    reach_ref, sigma_ref, show_ref, fold_ref, table_ref = refs[4:9]
    line, parts, top, reach, depth, inner = refs[9], refs[10:14], refs[14], refs[15:17], refs[17], refs[18]
    seq, hand = lax.axis_index("seq"), lax.axis_index("hand")
    tree_scalars(parent_ref, depth, inner)
    table_ref[0] = 1
    table_ref[S] = 0
    table_ref[2 * S] = 0
    for k, block in zip((0,) + FAR_LAST, blocks):
        base = 128 * jnp.bitwise_xor(seq, k)
        for half in range(2):
            start = base + 4 * jnp.bitwise_xor(hand, half)
            for r in range(4):
                line[pl.ds(start + r, 16, stride=8), :] = block[
                    half, :, 128 * r : 128 * r + 128
                ]

    def at(s):
        return pl.ds(pl.multiple_of(8 * s, 8), 8)

    for part in parts:
        part[...] = jnp.full(part.shape, -jnp.inf, F32)
    for s in range(1, S):
        part, up = parts[s % 4], at(parent_ref[s])
        part[up, :] = jnp.maximum(part[up, :], line[8 * s : 8 * s + 8, :])
    top[...] = jnp.maximum(
        jnp.maximum(parts[0][...], parts[1][...]), jnp.maximum(parts[2][...], parts[3][...])
    )
    for part in parts:
        part[...] = jnp.zeros(part.shape, F32)
    for s in range(1, S):
        part, up = parts[s % 4], at(parent_ref[s])
        raised = jnp.exp(line[8 * s : 8 * s + 8, :] - top[up, :])
        sigma_ref[8 * s : 8 * s + 8, :] = raised
        part[up, :] = part[up, :] + raised
    top[...] = (parts[0][...] + parts[1][...]) + (parts[2][...] + parts[3][...])
    one = jnp.ones((8, 128), F32)
    sigma_ref[0:8, :] = one
    for p in range(2):
        reach[p][0:8, :] = one
    zero = jnp.zeros((1, 128), F32)
    show_ref[0:1, :] = zero
    show_ref[S : S + 1, :] = zero
    fold_ref[0:1, :] = zero
    fold_ref[S : S + 1, :] = zero
    for s in range(1, S):
        up = at(parent_ref[s])
        sigma = sigma_ref[8 * s : 8 * s + 8, :] / top[up, :]
        sigma_ref[8 * s : 8 * s + 8, :] = sigma
        actor = (depth[s] + 1) & 1
        table_ref[s] = actor
        table_ref[S + s] = parent_ref[s]
        table_ref[2 * S + s] = pot_ref[s]
        for p in range(2):
            weight = jnp.where(actor == p, sigma, one)
            reach[p][8 * s : 8 * s + 8, :] = weight * reach[p][up, :]
        leaf = 1 - inner[s]
        folds = jnp.where(action_ref[s] == 0, leaf, 0)
        shows = (leaf - folds).astype(F32)
        folds = folds.astype(F32)
        for p in range(2):
            show_ref[p * S + s : p * S + s + 1, :] = jnp.full((1, 128), shows, F32)
            sign = jnp.where(actor == p, -folds, folds)
            fold_ref[p * S + s : p * S + s + 1, :] = jnp.full((1, 128), sign, F32)
    for p in range(2):
        for r in range(8):
            reach_ref[p * S : p * S + S, 128 * r : 128 * r + 128] = reach[1 - p][
                pl.ds(r, S, stride=8), :
            ].astype(BF)


def pieces(width):
    return [(a, min(a + 256, width)) for a in range(0, width, 256)]


def give(row, reach_ref, show, fold, gather_ref, code_ref, vcol, onehot, left, diag, ranks):
    rank_row = coded(row >> 16)
    ranks[...] = rank_row
    slot_row = coded(row & 65535).astype(BF)
    for a, b in pieces(HP):
        parts = []
        for c in range(a, b, 128):
            down = jnp.broadcast_to(rank_row[:, c : c + 128], (8, 128)).T
            vcol[c : c + 128, :] = jnp.broadcast_to(down[:, 0:1], (128, 128)).astype(BF)
            parts.append(
                jnp.where(slot_row[:, c : c + 128] == code_ref[...], jnp.ones((), BF), jnp.zeros((), BF))
            )
        part = jnp.concatenate(parts, axis=1)
        onehot[:, a:b] = part
        spread = jnp.dot(reach_ref[...], part, preferred_element_type=F32).astype(BF)
        for c in range(a, b, 128):
            part = spread[:, c - a : c - a + 128]
            left[:, c : c + 128] = part * show
            diag[:, c : c + 128] = part * fold
    cards = jnp.dot(diag[...], gather_ref[...], preferred_element_type=F32)
    high = cards.astype(BF).astype(F32)
    lane = lax.broadcasted_iota(jnp.int32, cards.shape, 1)
    left[:, HP:] = jnp.where(lane < 64, high, cards - high).astype(BF)


def settle(compat_ref, spread_ref, sums, vcol, onehot, left, diag, terms, ranks):
    rank_row = ranks[...].astype(BF)
    for a, b in pieces(HP):
        limit = compat_ref[:, a:b]
        gap = rank_row[:, a:b] - jnp.concatenate([vcol[...]] * ((b - a) // 128), axis=1)
        against = jnp.minimum(jnp.maximum(gap, -limit), limit)
        right = jnp.concatenate([against, spread_ref[:, a:b]], axis=0)
        chosen = jnp.dot(left[...], right, preferred_element_type=F32)
        chosen = chosen + diag[:, a:b].astype(F32)
        count = lax.broadcasted_iota(jnp.int32, chosen.shape, 0) == 0
        chosen = jnp.where(count, 1.0, chosen)
        high = chosen.astype(BF)
        terms[0 : 2 * S, a:b] = high
        terms[2 * S :, a:b] = (chosen - high.astype(F32)).astype(BF)
    for a, b in pieces(WIN):
        got = lax.dot_general(
            terms[...], onehot[a:b, :], (((1,), (1,)), ((), ())), preferred_element_type=F32
        )
        sums[:, a:b] = sums[:, a:b] + got[: 2 * S] + got[2 * S :]


def board_kernel(
    there_ref, table_ref, boards, reach_ref, sigma_ref, show_ref, fold_ref, fixed_any,
    mine_ref, theirs_ref, compat_ref, gather_ref, spread_ref, code_ref,
    sums, value0, value1, mine_list, sems, *buffers,
):
    pairs = [(fixed_any.at[pl.ds(0, WIN), pl.ds(HP + EXT, 128)], code_ref),
             (fixed_any.at[pl.ds(0, HP), pl.ds(HP, EXT)], gather_ref),
             (fixed_any.at[pl.ds(HP, EXT), pl.ds(0, HP)], spread_ref)]
    for a, b in pieces(HP):
        pairs.append((fixed_any.at[pl.ds(0, HP), pl.ds(a, b - a)], compat_ref.at[:, pl.ds(a, b - a)]))
    copies = [pltpu.make_async_copy(a, b, sems.at[i]) for i, (a, b) in enumerate(pairs)]
    for copy in copies:
        copy.start()
    sums[...] = jnp.zeros(sums.shape, F32)
    seq, hand = lax.axis_index("seq"), lax.axis_index("hand")

    kept, seen = jnp.int32(0), hand
    for i in range(4 * there_ref.shape[0]):
        flag = there_ref[i // 4, i % 4]
        both = flag & 1
        mine_list[kept] = i
        kept = kept + (flag >> 1) + (both & (1 - (seen & 1)))
        seen = seen + both

    show = show_ref[...].astype(BF)
    fold = fold_ref[...].astype(BF)

    def deal(i, turn=0):
        vcol, onehot, left, diag, terms, ranks = buffers[6 * turn : 6 * turn + 6]
        index = mine_list[i]
        give(boards[index >> 2, pl.ds(index & 3, 1), :], reach_ref, show, fold, gather_ref, code_ref,
             vcol, onehot, left, diag, ranks)

    for copy in copies[:2]:
        copy.wait()
    deal(0)
    for copy in copies[2:]:
        copy.wait()

    def add(turn=0):
        settle(compat_ref, spread_ref, sums, *buffers[6 * turn : 6 * turn + 6])

    @pl.when(kept > 0)
    def _():
        add()

    def step(i, carry):
        for turn in range(2):
            deal(1 + 2 * i + turn, turn)
            add(turn)
        return carry

    left_over = jnp.maximum(kept - 1, 0)
    lax.fori_loop(0, left_over >> 1, step, 0)

    @pl.when((left_over & 1) == 1)
    def _():
        deal(kept - 1)
        add()

    value = (value0, value1)
    for p in range(2):
        for r in range(8):
            value[p][pl.ds(r, S, stride=8), :] = sums[p * S : p * S + S, 128 * r : 128 * r + 128]

    def at(s):
        return pl.ds(pl.multiple_of(8 * s, 8), 8)

    def put(place, tile):
        turned = jnp.concatenate([tile[4:], tile[:4]], axis=0)
        tile = jnp.where(hand == 0, tile, turned)
        mine_ref[place] = tile[:4]
        theirs_ref[place] = tile[4:]

    mass = value[0][0:8, :]
    for k in range(4):
        put((k, pl.ds(192, 4)), mass)
    value[0][0:8, :] = jnp.zeros((8, 128), F32)
    for s in range(1, S):
        scale = table_ref[2 * S + s].astype(F32) / H
        for p in range(2):
            value[p][8 * s : 8 * s + 8, :] = value[p][8 * s : 8 * s + 8, :] * scale
    for s in range(S - 1, 0, -1):
        up = at(table_ref[S + s])
        sigma = sigma_ref[8 * s : 8 * s + 8, :]
        actor = table_ref[s]
        for p in range(2):
            own = value[p][8 * s : 8 * s + 8, :]
            value[p][up, :] = value[p][up, :] + jnp.where(actor == p, sigma, 1.0) * own
    for s in range(S):
        chunk = jnp.bitwise_xor(seq, s // 16)
        row = 4 * (s % 16)
        for p in range(2):
            put((chunk, pl.ds(64 * p + row, 4)), value[p][8 * s : 8 * s + 8, :])
        if s == 0:
            put((chunk, pl.ds(128 + row, 4)), jnp.zeros((8, 128), F32))
        else:
            up = at(table_ref[S + s])
            actor = table_ref[s]
            own = jnp.where(actor == 0, value[0][8 * s : 8 * s + 8, :], value[1][8 * s : 8 * s + 8, :])
            over = jnp.where(actor == 0, value[0][up, :], value[1][up, :])
            put((chunk, pl.ds(128 + row, 4)), own - over)


def finish_kernel(logits_ref, mine, got, c1, c2, c3, new_ref, values_ref, total):
    total[...] = ((mine[0] + got[0]) + c1[...]) + (c2[...] + c3[...])
    for r in range(4):
        mass = total[192 + r : 193 + r, :] + 1.0
        lanes = slice(128 * r, 128 * r + 128)
        for p in range(2):
            values_ref[p, :, lanes] = total[pl.ds(64 * p + r, 16, stride=4), :] / mass
        gain = total[pl.ds(128 + r, 16, stride=4), :] / mass
        new_ref[:, lanes] = logits_ref[:, lanes] + STEP * gain


def swap(x, axis, size, bits):
    return lax.ppermute(x, axis, [(i, i ^ bits) for i in range(size)])


def local(board_cards, ranks, buckets, parent, action, pot, logits):
    sds = jax.ShapeDtypeStruct
    pair, fixed = constants()
    groups, planes = lax.axis_size("boards"), 8
    boards = board_cards.shape[0]
    slots = boards // planes
    other = swap(logits, "hand", 2, 1)
    own = pl.pallas_call(
        prep_kernel,
        compiler_params=pltpu.CompilerParams(vmem_limit_bytes=60 * 2**20),
        out_shape=sds((groups, slots, HP), jnp.int32),
        in_specs=[VM, VM, VM, VM],
        out_specs=VM,
        cost_estimate=pl.CostEstimate(flops=4_000_000_000, bytes_accessed=2_000_000, transcendentals=0),
        scratch_shapes=[pltpu.VMEM((boards, HQ), jnp.int32)],
    )(board_cards.T, ranks, buckets, jnp.asarray(pair))
    own, other = lax.optimization_barrier((own, other))
    wide = jnp.stack([logits, other])
    packs = lax.all_to_all(own, "boards", 0, 0)
    blocks = [wide] + [swap(wide, "seq", 4, k) for k in FAR_LAST]
    reach, sigma, show, fold, table = pl.pallas_call(
        reach_kernel,
        compiler_params=pltpu.CompilerParams(vmem_limit_bytes=8 * 2**20),
        out_shape=[sds((2 * S, WIN), BF), sds((8 * S, 128), F32), sds((2 * S, 128), F32),
                   sds((2 * S, 128), F32), sds((3 * S,), jnp.int32)],
        in_specs=[SM] * 3 + [VM] * 4,
        out_specs=[VM] * 4 + [SM],
        scratch_shapes=[
            pltpu.VMEM((8 * S, 128), F32),
            *[pltpu.VMEM((4 * S, 128), F32)] * 5,
            *[pltpu.VMEM((8 * S, 128), F32)] * 2,
            pltpu.SMEM((S,), jnp.int32),
            pltpu.SMEM((S,), jnp.int32),
        ],
        cost_estimate=pl.CostEstimate(flops=4_000_000, bytes_accessed=2_000_000, transcendentals=65536),
    )(parent, action, pot, *blocks)
    there = packs[:, :, LIVE] >> 16
    mine, theirs = pl.pallas_call(
        board_kernel,
        out_shape=[sds((4, 200, 128), F32)] * 2,
        in_specs=[SM] * 2 + [VM] * 5 + [AN],
        out_specs=[VM] * 2,
        scratch_shapes=[
            pltpu.VMEM((HP, HP), BF),
            pltpu.VMEM((HP, EXT), BF),
            pltpu.VMEM((EXT, HP), BF),
            pltpu.VMEM((WIN, 128), BF),
            pltpu.VMEM((2 * S, WIN), F32),
            *[pltpu.VMEM((8 * S, 128), F32)] * 2,
            pltpu.SMEM((groups * slots + 8,), jnp.int32),
            pltpu.SemaphoreType.DMA((8,)),
            *[
                pltpu.VMEM((HP, 128), BF),
                pltpu.VMEM((WIN, HP), BF),
                pltpu.VMEM((2 * S, HP + EXT), BF),
                pltpu.VMEM((2 * S, HP), BF),
                pltpu.VMEM((4 * S, HP), BF),
                pltpu.VMEM((1, HP), F32),
            ]
            * 2,
        ],
        compiler_params=pltpu.CompilerParams(vmem_limit_bytes=50 * 2**20),
        cost_estimate=pl.CostEstimate(flops=8_000_000_000, bytes_accessed=8_000_000, transcendentals=0),
    )(there, table, packs, reach, sigma, show, fold, jnp.asarray(fixed))
    got = swap(theirs, "hand", 2, 1)
    chunks = [swap(mine[k] + got[k], "seq", 4, k) for k in FAR_LAST]
    new_logits, values = pl.pallas_call(
        finish_kernel,
        compiler_params=pltpu.CompilerParams(vmem_limit_bytes=8 * 2**20),
        out_shape=[sds(logits.shape, F32), sds((2,) + logits.shape, F32)],
        in_specs=[VM] * 6,
        out_specs=[VM] * 2,
        scratch_shapes=[pltpu.VMEM((200, 128), F32)],
    )(logits, mine, got, *chunks)
    return new_logits, values


def solution(mesh):
    return jax.shard_map(
        local,
        mesh=mesh,
        in_specs=(
            P("boards", None),
            P("boards", None),
            P("boards", None),
            P(),
            P(),
            P(),
            P("seq", ("boards", "hand")),
        ),
        out_specs=(P("seq", ("boards", "hand")), P(None, "seq", ("boards", "hand"))),
        check_vma=False,
    )
```

```python
import functools

import jax
import jax.numpy as jnp
import ml_dtypes
import numpy as np
from jax import lax
from jax.experimental import pallas as pl
from jax.experimental.pallas import tpu as pltpu
from jax.sharding import PartitionSpec as P

CARDS = 52
FREE = CARDS - 5
S = 64
WIN = 1024
H = CARDS * (CARDS - 1) // 2
LIVE = FREE * (FREE - 1) // 2
HQ = 1408
HP = 1152
EXT = 128
DEAD = 2047
STEP = 0.5
FAR_LAST = (1, 3, 2)
BF = jnp.bfloat16
F32 = jnp.float32
VM = pl.BlockSpec(memory_space=pltpu.VMEM)
SM = pl.BlockSpec(memory_space=pltpu.SMEM)
AN = pl.BlockSpec(memory_space=pl.ANY)


def constants():
    pair = np.full((2, HQ), CARDS, np.int32)
    pair[:, :H] = np.triu_indices(CARDS, 1)
    first, second = np.triu_indices(FREE, 1)
    held = np.zeros((HP, 64), np.float32)
    held[np.arange(LIVE), first] = 1
    held[np.arange(LIVE), second] = 1
    compat = np.zeros((HP, HP), np.float32)
    compat[:LIVE, :LIVE] = (held @ held.T)[:LIVE, :LIVE] == 0
    held[:LIVE, FREE] = 1
    gather = np.concatenate([held, held], axis=1)
    held[:, :FREE] *= -1
    spread = np.concatenate([held, held], axis=1).T
    k = np.arange(WIN)
    code = np.broadcast_to(((128 + k % 128) * 2.0 ** (k // 128))[:, None], (WIN, 128))
    code = np.pad(code, ((0, HP - WIN), (0, 0)))
    fixed = np.concatenate([compat, gather, code], axis=1)
    fixed = np.concatenate([fixed, np.pad(spread, ((0, 0), (0, EXT + 128)))], axis=0)
    return pair, np.asarray(fixed, ml_dtypes.bfloat16)


def coded(value):
    power = jnp.ones(value.shape, F32)
    for bit in range(6):
        on = (value >> (7 + bit)) & 1
        power = power * jnp.where(on == 1, float(2 ** (2**bit)), 1.0)
    return ((value & 127) + 128).astype(F32) * power


def prep_kernel(cards_ref, ranks_ref, buckets_ref, pair_ref, out_ref, wide):
    boards = buckets_ref.shape[0]
    wide[:, 0:H] = ranks_ref[...] * 2048 + (buckets_ref[...] & (WIN - 1))
    lanes = lax.broadcasted_iota(jnp.int32, (1, HQ), 1)
    row = lax.broadcasted_iota(jnp.int32, (boards, boards), 0)
    col = lax.broadcasted_iota(jnp.int32, (boards, boards), 1)

    def across(key):
        return jnp.sum(jnp.where(row == col, key.astype(F32), 0.0), axis=0, keepdims=True)

    def down(key):
        return jnp.sum(jnp.where(row == col, key.astype(F32), 0.0), axis=1, keepdims=True).astype(jnp.int32)

    first, second = pair_ref[0:1, :], pair_ref[1:2, :]
    low, high = first, second
    dead = lanes >= H
    for c in range(5):
        card = down(cards_ref[c : c + 1, :])
        dead = dead | (first == card) | (second == card)
        low = low - jnp.where(card < first, 1, 0)
        high = high - jnp.where(card < second, 1, 0)
    shift = lanes - (((low * (2 * FREE - 1 - low)) >> 1) + high - low - 1)
    word = jnp.where(dead, DEAD, (wide[...] & 0xFFFFFF) + (shift << 24))
    for bit in range(8):
        moved = pltpu.roll(word, HQ - (1 << bit), 1)
        mark = jnp.int32(-(2**31) if bit == 7 else 2 ** (24 + bit))
        word = jnp.where(moved & mark != 0, moved, jnp.where(word & mark != 0, DEAD, word))
    seq, hand = lax.axis_index("seq"), lax.axis_index("hand")
    group = lax.axis_index("boards")
    cluster = buckets_ref[:, 0:1] // WIN
    same = across(cluster) == cluster.astype(F32)

    def count(mask):
        return jnp.sum(jnp.where(mask, 1.0, 0.0), axis=1, keepdims=True).astype(jnp.int32)

    twins = count(same & (col < row))
    few = count(same) <= 16
    turn = cluster + (group >> 1) + twins
    ours = jnp.where(few, turn & 3, turn & 7) == jnp.where(few, seq, seq + 4 * hand)
    slots = out_ref.shape[1]
    slot = jnp.where(ours, slots * cluster + jnp.where(few, twins >> 2, twins >> 3), -1)
    flag = jnp.where(few, 1, 2)
    word = jnp.where(lanes[:, :HP] < LIVE, word[:, :HP] & 0xFFFFFF, 2048 * flag + DEAD)
    taken = lax.broadcasted_iota(jnp.int32, (slots * out_ref.shape[0], boards), 0).astype(F32) == across(slot)
    taken = jnp.where(taken, 1.0, 0.0).astype(BF)

    def deal(shift):
        part = ((word >> shift) & 255).astype(F32).astype(BF)
        return jnp.dot(taken, part, preferred_element_type=F32).astype(jnp.int32)

    word = deal(0) + (deal(8) << 8) + (deal(16) << 16)
    word = ((word >> 11) << 16) + (word & 2047)
    for c in range(out_ref.shape[0]):
        out_ref[c] = word[slots * c : slots * c + slots, :]


def tree_scalars(parent_ref, depth, inner):
    depth[0] = 0
    for s in range(S):
        inner[s] = 0
    for s in range(1, S):
        up = parent_ref[s]
        depth[s] = depth[up] + 1
        inner[up] = 1


def tree_kernel(parent_ref, action_ref, pot_ref, wide_any, show_ref, fold_ref, table_ref, depth, inner):
    tree_scalars(parent_ref, depth, inner)
    table_ref[0] = 1
    table_ref[S] = 0
    table_ref[2 * S] = 0
    zero = jnp.zeros((1, 128), F32)
    show_ref[0:1, :] = zero
    show_ref[S : S + 1, :] = zero
    fold_ref[0:1, :] = zero
    fold_ref[S : S + 1, :] = zero
    for s in range(1, S):
        actor = (depth[s] + 1) & 1
        table_ref[s] = actor
        table_ref[S + s] = parent_ref[s]
        table_ref[2 * S + s] = pot_ref[s]
        leaf = 1 - inner[s]
        folds = jnp.where(action_ref[s] == 0, leaf, 0)
        shows = (leaf - folds).astype(F32)
        folds = folds.astype(F32)
        for p in range(2):
            show_ref[p * S + s : p * S + s + 1, :] = jnp.full((1, 128), shows, F32)
            sign = jnp.where(actor == p, -folds, folds)
            fold_ref[p * S + s : p * S + s + 1, :] = jnp.full((1, 128), sign, F32)


def reach_kernel(table_ref, *refs):
    blocks = refs[:4]
    reach_ref, sigma_ref = refs[4:6]
    line, parts, top, reach = refs[6], refs[7:11], refs[11], refs[12:14]
    seq, hand = lax.axis_index("seq"), lax.axis_index("hand")
    for k, block in zip((0,) + FAR_LAST, blocks):
        base = 128 * jnp.bitwise_xor(seq, k)
        for half in range(2):
            start = base + 4 * jnp.bitwise_xor(hand, half)
            for r in range(4):
                line[pl.ds(start + r, 16, stride=8), :] = block[
                    half, :, 128 * r : 128 * r + 128
                ]

    def at(s):
        return pl.ds(pl.multiple_of(8 * s, 8), 8)

    for part in parts:
        part[...] = jnp.full(part.shape, -jnp.inf, F32)
    for s in range(1, S):
        part, up = parts[s % 4], at(table_ref[S + s])
        part[up, :] = jnp.maximum(part[up, :], line[8 * s : 8 * s + 8, :])
    top[...] = jnp.maximum(
        jnp.maximum(parts[0][...], parts[1][...]), jnp.maximum(parts[2][...], parts[3][...])
    )
    for part in parts:
        part[...] = jnp.zeros(part.shape, F32)
    for s in range(1, S):
        part, up = parts[s % 4], at(table_ref[S + s])
        raised = jnp.exp(line[8 * s : 8 * s + 8, :] - top[up, :])
        sigma_ref[8 * s : 8 * s + 8, :] = raised
        part[up, :] = part[up, :] + raised
    top[...] = (parts[0][...] + parts[1][...]) + (parts[2][...] + parts[3][...])
    one = jnp.ones((8, 128), F32)
    sigma_ref[0:8, :] = one
    for p in range(2):
        reach[p][0:8, :] = one
    for s in range(1, S):
        up = at(table_ref[S + s])
        sigma = sigma_ref[8 * s : 8 * s + 8, :] / top[up, :]
        sigma_ref[8 * s : 8 * s + 8, :] = sigma
        actor = table_ref[s]
        for p in range(2):
            weight = jnp.where(actor == p, sigma, one)
            reach[p][8 * s : 8 * s + 8, :] = weight * reach[p][up, :]
    for p in range(2):
        for r in range(8):
            reach_ref[p * S : p * S + S, 128 * r : 128 * r + 128] = reach[1 - p][
                pl.ds(r, S, stride=8), :
            ].astype(BF)


def pieces(width):
    return [(a, min(a + 256, width)) for a in range(0, width, 256)]


def give(row, reach_ref, show, fold, gather_ref, code_ref, vcol, onehot, left, diag, ranks):
    rank_row = coded(row >> 16)
    ranks[...] = rank_row
    slot_row = coded(row & 65535).astype(BF)
    for a, b in pieces(HP):
        parts = []
        for c in range(a, b, 128):
            down = jnp.broadcast_to(rank_row[:, c : c + 128], (8, 128)).T
            vcol[c : c + 128, :] = jnp.broadcast_to(down[:, 0:1], (128, 128)).astype(BF)
            parts.append(
                jnp.where(slot_row[:, c : c + 128] == code_ref[...], jnp.ones((), BF), jnp.zeros((), BF))
            )
        part = jnp.concatenate(parts, axis=1)
        onehot[:, a:b] = part
        spread = jnp.dot(reach_ref[...], part, preferred_element_type=F32).astype(BF)
        for c in range(a, b, 128):
            part = spread[:, c - a : c - a + 128]
            left[:, c : c + 128] = part * show
            diag[:, c : c + 128] = part * fold
    cards = jnp.dot(diag[...], gather_ref[...], preferred_element_type=F32)
    high = cards.astype(BF).astype(F32)
    lane = lax.broadcasted_iota(jnp.int32, cards.shape, 1)
    left[:, HP:] = jnp.where(lane < 64, high, cards - high).astype(BF)


def settle(compat_ref, spread_ref, sums, vcol, onehot, left, diag, terms, ranks):
    rank_row = ranks[...].astype(BF)
    for a, b in pieces(HP):
        limit = compat_ref[:, a:b]
        gap = rank_row[:, a:b] - jnp.concatenate([vcol[...]] * ((b - a) // 128), axis=1)
        against = jnp.minimum(jnp.maximum(gap, -limit), limit)
        right = jnp.concatenate([against, spread_ref[:, a:b]], axis=0)
        chosen = jnp.dot(left[...], right, preferred_element_type=F32)
        chosen = chosen + diag[:, a:b].astype(F32)
        count = lax.broadcasted_iota(jnp.int32, chosen.shape, 0) == 0
        chosen = jnp.where(count, 1.0, chosen)
        high = chosen.astype(BF)
        terms[0 : 2 * S, a:b] = high
        terms[2 * S :, a:b] = (chosen - high.astype(F32)).astype(BF)
    for a, b in pieces(WIN):
        got = lax.dot_general(
            terms[...], onehot[a:b, :], (((1,), (1,)), ((), ())), preferred_element_type=F32
        )
        sums[:, a:b] = sums[:, a:b] + got[: 2 * S] + got[2 * S :]


def board_kernel(
    there_ref, table_ref, boards, reach_ref, sigma_ref, show_ref, fold_ref, fixed_any,
    mine_ref, theirs_ref, compat_ref, gather_ref, spread_ref, code_ref,
    sums, value0, value1, mine_list, sems, *buffers,
):
    pairs = [(fixed_any.at[pl.ds(0, WIN), pl.ds(HP + EXT, 128)], code_ref),
             (fixed_any.at[pl.ds(0, HP), pl.ds(HP, EXT)], gather_ref),
             (fixed_any.at[pl.ds(HP, EXT), pl.ds(0, HP)], spread_ref)]
    for a, b in pieces(HP):
        pairs.append((fixed_any.at[pl.ds(0, HP), pl.ds(a, b - a)], compat_ref.at[:, pl.ds(a, b - a)]))
    copies = [pltpu.make_async_copy(a, b, sems.at[i]) for i, (a, b) in enumerate(pairs)]
    for copy in copies:
        copy.start()
    sums[...] = jnp.zeros(sums.shape, F32)
    seq, hand = lax.axis_index("seq"), lax.axis_index("hand")

    kept, seen = jnp.int32(0), hand
    for i in range(4 * there_ref.shape[0]):
        flag = there_ref[i // 4, i % 4]
        both = flag & 1
        mine_list[kept] = i
        kept = kept + (flag >> 1) + (both & (1 - (seen & 1)))
        seen = seen + both

    show = show_ref[...].astype(BF)
    fold = fold_ref[...].astype(BF)

    def deal(i, turn=0):
        vcol, onehot, left, diag, terms, ranks = buffers[6 * turn : 6 * turn + 6]
        index = mine_list[i]
        give(boards[index >> 2, pl.ds(index & 3, 1), :], reach_ref, show, fold, gather_ref, code_ref,
             vcol, onehot, left, diag, ranks)

    for copy in copies[:2]:
        copy.wait()
    deal(0)
    for copy in copies[2:]:
        copy.wait()

    def add(turn=0):
        settle(compat_ref, spread_ref, sums, *buffers[6 * turn : 6 * turn + 6])

    @pl.when(kept > 0)
    def _():
        add()

    def step(i, carry):
        for turn in range(2):
            deal(1 + 2 * i + turn, turn)
            add(turn)
        return carry

    left_over = jnp.maximum(kept - 1, 0)
    lax.fori_loop(0, left_over >> 1, step, 0)

    @pl.when((left_over & 1) == 1)
    def _():
        deal(kept - 1)
        add()

    value = (value0, value1)
    for p in range(2):
        for r in range(8):
            value[p][pl.ds(r, S, stride=8), :] = sums[p * S : p * S + S, 128 * r : 128 * r + 128]

    def at(s):
        return pl.ds(pl.multiple_of(8 * s, 8), 8)

    def put(place, tile):
        turned = jnp.concatenate([tile[4:], tile[:4]], axis=0)
        tile = jnp.where(hand == 0, tile, turned)
        mine_ref[place] = tile[:4]
        theirs_ref[place] = tile[4:]

    mass = value[0][0:8, :]
    for k in range(4):
        put((k, pl.ds(192, 4)), mass)
    value[0][0:8, :] = jnp.zeros((8, 128), F32)
    for s in range(1, S):
        scale = table_ref[2 * S + s].astype(F32) / H
        for p in range(2):
            value[p][8 * s : 8 * s + 8, :] = value[p][8 * s : 8 * s + 8, :] * scale
    for s in range(S - 1, 0, -1):
        up = at(table_ref[S + s])
        sigma = sigma_ref[8 * s : 8 * s + 8, :]
        actor = table_ref[s]
        for p in range(2):
            own = value[p][8 * s : 8 * s + 8, :]
            value[p][up, :] = value[p][up, :] + jnp.where(actor == p, sigma, 1.0) * own
    for s in range(S):
        chunk = jnp.bitwise_xor(seq, s // 16)
        row = 4 * (s % 16)
        for p in range(2):
            put((chunk, pl.ds(64 * p + row, 4)), value[p][8 * s : 8 * s + 8, :])
        if s == 0:
            put((chunk, pl.ds(128 + row, 4)), jnp.zeros((8, 128), F32))
        else:
            up = at(table_ref[S + s])
            actor = table_ref[s]
            own = jnp.where(actor == 0, value[0][8 * s : 8 * s + 8, :], value[1][8 * s : 8 * s + 8, :])
            over = jnp.where(actor == 0, value[0][up, :], value[1][up, :])
            put((chunk, pl.ds(128 + row, 4)), own - over)


def finish_kernel(logits_ref, mine, got, c1, c2, c3, new_ref, values_ref, total):
    total[...] = ((mine[0] + got[0]) + c1[...]) + (c2[...] + c3[...])
    for r in range(4):
        mass = total[192 + r : 193 + r, :] + 1.0
        lanes = slice(128 * r, 128 * r + 128)
        for p in range(2):
            values_ref[p, :, lanes] = total[pl.ds(64 * p + r, 16, stride=4), :] / mass
        gain = total[pl.ds(128 + r, 16, stride=4), :] / mass
        new_ref[:, lanes] = logits_ref[:, lanes] + STEP * gain


def swap(x, axis, size, bits):
    return lax.ppermute(x, axis, [(i, i ^ bits) for i in range(size)])


def local(board_cards, ranks, buckets, parent, action, pot, logits):
    sds = jax.ShapeDtypeStruct
    pair, fixed = constants()
    groups, planes = lax.axis_size("boards"), 8
    boards = board_cards.shape[0]
    slots = boards // planes
    other = swap(logits, "hand", 2, 1)
    own = pl.pallas_call(
        prep_kernel,
        compiler_params=pltpu.CompilerParams(vmem_limit_bytes=60 * 2**20),
        out_shape=sds((groups, slots, HP), jnp.int32),
        in_specs=[VM, VM, VM, VM],
        out_specs=VM,
        cost_estimate=pl.CostEstimate(flops=4_000_000_000, bytes_accessed=2_000_000, transcendentals=0),
        scratch_shapes=[pltpu.VMEM((boards, HQ), jnp.int32)],
    )(board_cards.T, ranks, buckets, jnp.asarray(pair))
    own, other = lax.optimization_barrier((own, other))
    wide = jnp.stack([logits, other])
    packs = lax.all_to_all(own, "boards", 0, 0)
    blocks = [wide] + [swap(wide, "seq", 4, k) for k in FAR_LAST]
    small = pltpu.CompilerParams(vmem_limit_bytes=8 * 2**20)
    show, fold, table = pl.pallas_call(
        tree_kernel,
        compiler_params=small,
        out_shape=[sds((2 * S, 128), F32), sds((2 * S, 128), F32), sds((3 * S,), jnp.int32)],
        in_specs=[SM] * 3 + [AN],
        out_specs=[VM, VM, SM],
        scratch_shapes=[pltpu.SMEM((S,), jnp.int32)] * 2,
        cost_estimate=pl.CostEstimate(flops=1_000_000_000, bytes_accessed=2_000_000, transcendentals=0),
    )(parent, action, pot, wide)
    reach, sigma = pl.pallas_call(
        reach_kernel,
        compiler_params=small,
        out_shape=[sds((2 * S, WIN), BF), sds((8 * S, 128), F32)],
        in_specs=[SM] + [VM] * 4,
        out_specs=[VM] * 2,
        scratch_shapes=[
            pltpu.VMEM((8 * S, 128), F32),
            *[pltpu.VMEM((4 * S, 128), F32)] * 5,
            *[pltpu.VMEM((8 * S, 128), F32)] * 2,
        ],
        cost_estimate=pl.CostEstimate(flops=4_000_000, bytes_accessed=2_000_000, transcendentals=65536),
    )(table, *blocks)
    there = packs[:, :, LIVE] >> 16
    mine, theirs = pl.pallas_call(
        board_kernel,
        out_shape=[sds((4, 200, 128), F32)] * 2,
        in_specs=[SM] * 2 + [VM] * 5 + [AN],
        out_specs=[VM] * 2,
        scratch_shapes=[
            pltpu.VMEM((HP, HP), BF),
            pltpu.VMEM((HP, EXT), BF),
            pltpu.VMEM((EXT, HP), BF),
            pltpu.VMEM((WIN, 128), BF),
            pltpu.VMEM((2 * S, WIN), F32),
            *[pltpu.VMEM((8 * S, 128), F32)] * 2,
            pltpu.SMEM((groups * slots + 8,), jnp.int32),
            pltpu.SemaphoreType.DMA((8,)),
            *[
                pltpu.VMEM((HP, 128), BF),
                pltpu.VMEM((WIN, HP), BF),
                pltpu.VMEM((2 * S, HP + EXT), BF),
                pltpu.VMEM((2 * S, HP), BF),
                pltpu.VMEM((4 * S, HP), BF),
                pltpu.VMEM((1, HP), F32),
            ]
            * 2,
        ],
        compiler_params=pltpu.CompilerParams(vmem_limit_bytes=50 * 2**20),
        cost_estimate=pl.CostEstimate(flops=8_000_000_000, bytes_accessed=8_000_000, transcendentals=0),
    )(there, table, packs, reach, sigma, show, fold, jnp.asarray(fixed))
    got = swap(theirs, "hand", 2, 1)
    chunks = [swap(mine[k] + got[k], "seq", 4, k) for k in FAR_LAST]
    new_logits, values = pl.pallas_call(
        finish_kernel,
        compiler_params=pltpu.CompilerParams(vmem_limit_bytes=8 * 2**20),
        out_shape=[sds(logits.shape, F32), sds((2,) + logits.shape, F32)],
        in_specs=[VM] * 6,
        out_specs=[VM] * 2,
        scratch_shapes=[pltpu.VMEM((200, 128), F32)],
    )(logits, mine, got, *chunks)
    return new_logits, values


def solution(mesh):
    return jax.shard_map(
        local,
        mesh=mesh,
        in_specs=(
            P("boards", None),
            P("boards", None),
            P("boards", None),
            P(),
            P(),
            P(),
            P("seq", ("boards", "hand")),
        ),
        out_specs=(P("seq", ("boards", "hand")), P(None, "seq", ("boards", "hand"))),
        check_vma=False,
    )
```

```python
import functools

import jax
import jax.numpy as jnp
import ml_dtypes
import numpy as np
from jax import lax
from jax.experimental import pallas as pl
from jax.experimental.pallas import tpu as pltpu
from jax.sharding import PartitionSpec as P

CARDS = 52
FREE = CARDS - 5
S = 64
WIN = 1024
H = CARDS * (CARDS - 1) // 2
LIVE = FREE * (FREE - 1) // 2
HQ = 1408
HP = 1152
EXT = 128
DEAD = 2047
STEP = 0.5
FAR_LAST = (1, 3, 2)
BF = jnp.bfloat16
F32 = jnp.float32
VM = pl.BlockSpec(memory_space=pltpu.VMEM)
SM = pl.BlockSpec(memory_space=pltpu.SMEM)
AN = pl.BlockSpec(memory_space=pl.ANY)


def constants():
    pair = np.full((2, HQ), CARDS, np.int32)
    pair[:, :H] = np.triu_indices(CARDS, 1)
    first, second = np.triu_indices(FREE, 1)
    held = np.zeros((HP, 64), np.float32)
    held[np.arange(LIVE), first] = 1
    held[np.arange(LIVE), second] = 1
    compat = np.zeros((HP, HP), np.float32)
    compat[:LIVE, :LIVE] = (held @ held.T)[:LIVE, :LIVE] == 0
    held[:LIVE, FREE] = 1
    gather = np.concatenate([held, held], axis=1)
    held[:, :FREE] *= -1
    spread = np.concatenate([held, held], axis=1).T
    k = np.arange(WIN)
    code = np.broadcast_to(((128 + k % 128) * 2.0 ** (k // 128))[:, None], (WIN, 128))
    code = np.pad(code, ((0, HP - WIN), (0, 0)))
    fixed = np.concatenate([compat, gather, code], axis=1)
    fixed = np.concatenate([fixed, np.pad(spread, ((0, 0), (0, EXT + 128)))], axis=0)
    return pair, np.asarray(fixed, ml_dtypes.bfloat16)


def coded(value):
    power = jnp.ones(value.shape, F32)
    for bit in range(6):
        on = (value >> (7 + bit)) & 1
        power = power * jnp.where(on == 1, float(2 ** (2**bit)), 1.0)
    return ((value & 127) + 128).astype(F32) * power


def prep_kernel(cards_ref, ranks_ref, buckets_ref, pair_ref, out_ref, wide):
    boards = buckets_ref.shape[0]
    wide[:, 0:H] = ranks_ref[...] * 2048 + (buckets_ref[...] & (WIN - 1))
    lanes = lax.broadcasted_iota(jnp.int32, (1, HQ), 1)
    row = lax.broadcasted_iota(jnp.int32, (boards, boards), 0)
    col = lax.broadcasted_iota(jnp.int32, (boards, boards), 1)

    def across(key):
        return jnp.sum(jnp.where(row == col, key.astype(F32), 0.0), axis=0, keepdims=True)

    def down(key):
        return jnp.sum(jnp.where(row == col, key.astype(F32), 0.0), axis=1, keepdims=True).astype(jnp.int32)

    first, second = pair_ref[0:1, :], pair_ref[1:2, :]
    low, high = first, second
    dead = lanes >= H
    for c in range(5):
        card = down(cards_ref[c : c + 1, :])
        dead = dead | (first == card) | (second == card)
        low = low - jnp.where(card < first, 1, 0)
        high = high - jnp.where(card < second, 1, 0)
    shift = lanes - (((low * (2 * FREE - 1 - low)) >> 1) + high - low - 1)
    word = jnp.where(dead, DEAD, (wide[...] & 0xFFFFFF) + (shift << 24))
    for bit in range(8):
        moved = pltpu.roll(word, HQ - (1 << bit), 1)
        mark = jnp.int32(-(2**31) if bit == 7 else 2 ** (24 + bit))
        word = jnp.where(moved & mark != 0, moved, jnp.where(word & mark != 0, DEAD, word))
    seq, hand = lax.axis_index("seq"), lax.axis_index("hand")
    group = lax.axis_index("boards")
    cluster = buckets_ref[:, 0:1] // WIN
    same = across(cluster) == cluster.astype(F32)

    def count(mask):
        return jnp.sum(jnp.where(mask, 1.0, 0.0), axis=1, keepdims=True).astype(jnp.int32)

    twins = count(same & (col < row))
    few = count(same) <= 16
    turn = cluster + (group >> 1) + twins
    ours = jnp.where(few, turn & 3, turn & 7) == jnp.where(few, seq, seq + 4 * hand)
    slots = out_ref.shape[1]
    slot = jnp.where(ours, slots * cluster + jnp.where(few, twins >> 2, twins >> 3), -1)
    flag = jnp.where(few, 1, 2)
    word = jnp.where(lanes[:, :HP] < LIVE, word[:, :HP] & 0xFFFFFF, 2048 * flag + DEAD)
    taken = lax.broadcasted_iota(jnp.int32, (slots * out_ref.shape[0], boards), 0).astype(F32) == across(slot)
    taken = jnp.where(taken, 1.0, 0.0).astype(BF)

    def deal(shift):
        part = ((word >> shift) & 255).astype(F32).astype(BF)
        return jnp.dot(taken, part, preferred_element_type=F32).astype(jnp.int32)

    word = deal(0) + (deal(8) << 8) + (deal(16) << 16)
    word = ((word >> 11) << 16) + (word & 2047)
    for c in range(out_ref.shape[0]):
        out_ref[c] = word[slots * c : slots * c + slots, :]


def tree_scalars(parent_ref, depth, inner):
    depth[0] = 0
    for s in range(S):
        inner[s] = 0
    for s in range(1, S):
        up = parent_ref[s]
        depth[s] = depth[up] + 1
        inner[up] = 1


def tree_kernel(parent_ref, action_ref, pot_ref, wide_any, show_ref, fold_ref, table_ref, depth, inner):
    tree_scalars(parent_ref, depth, inner)
    table_ref[0] = 1
    table_ref[S] = 0
    table_ref[2 * S] = 0
    zero = jnp.zeros((1, 128), F32)
    show_ref[0:1, :] = zero
    show_ref[S : S + 1, :] = zero
    fold_ref[0:1, :] = zero
    fold_ref[S : S + 1, :] = zero
    for s in range(1, S):
        actor = (depth[s] + 1) & 1
        table_ref[s] = actor
        table_ref[S + s] = parent_ref[s]
        table_ref[2 * S + s] = pot_ref[s]
        leaf = 1 - inner[s]
        folds = jnp.where(action_ref[s] == 0, leaf, 0)
        shows = (leaf - folds).astype(F32)
        folds = folds.astype(F32)
        for p in range(2):
            show_ref[p * S + s : p * S + s + 1, :] = jnp.full((1, 128), shows, F32)
            sign = jnp.where(actor == p, -folds, folds)
            fold_ref[p * S + s : p * S + s + 1, :] = jnp.full((1, 128), sign, F32)


def reach_kernel(table_ref, *refs):
    blocks = refs[:4]
    reach_ref, sigma_ref = refs[4:6]
    line, parts, top, reach = refs[6], refs[7:11], refs[11], refs[12:14]
    seq, hand = lax.axis_index("seq"), lax.axis_index("hand")
    for k, block in zip((0,) + FAR_LAST, blocks):
        base = 128 * jnp.bitwise_xor(seq, k)
        for half in range(2):
            start = base + 4 * jnp.bitwise_xor(hand, half)
            for r in range(4):
                line[pl.ds(start + r, 16, stride=8), :] = block[
                    half, :, 128 * r : 128 * r + 128
                ]

    def at(s):
        return pl.ds(pl.multiple_of(8 * s, 8), 8)

    for part in parts:
        part[...] = jnp.full(part.shape, -jnp.inf, F32)
    for s in range(1, S):
        part, up = parts[s % 4], at(table_ref[S + s])
        part[up, :] = jnp.maximum(part[up, :], line[8 * s : 8 * s + 8, :])
    top[...] = jnp.maximum(
        jnp.maximum(parts[0][...], parts[1][...]), jnp.maximum(parts[2][...], parts[3][...])
    )
    for part in parts:
        part[...] = jnp.zeros(part.shape, F32)
    for s in range(1, S):
        part, up = parts[s % 4], at(table_ref[S + s])
        raised = jnp.exp(line[8 * s : 8 * s + 8, :] - top[up, :])
        sigma_ref[8 * s : 8 * s + 8, :] = raised
        part[up, :] = part[up, :] + raised
    top[...] = (parts[0][...] + parts[1][...]) + (parts[2][...] + parts[3][...])
    one = jnp.ones((8, 128), F32)
    sigma_ref[0:8, :] = one
    for p in range(2):
        reach[p][0:8, :] = one
    for s in range(1, S):
        up = at(table_ref[S + s])
        sigma = sigma_ref[8 * s : 8 * s + 8, :] / top[up, :]
        sigma_ref[8 * s : 8 * s + 8, :] = sigma
        actor = table_ref[s]
        for p in range(2):
            weight = jnp.where(actor == p, sigma, one)
            reach[p][8 * s : 8 * s + 8, :] = weight * reach[p][up, :]
    for p in range(2):
        for r in range(8):
            reach_ref[p * S : p * S + S, 128 * r : 128 * r + 128] = reach[1 - p][
                pl.ds(r, S, stride=8), :
            ].astype(BF)


def pieces(width):
    return [(a, min(a + 256, width)) for a in range(0, width, 256)]


def give(row, reach_ref, show, fold, gather_ref, code_ref, vcol, onehot, left, diag, ranks):
    rank_row = coded(row >> 16)
    ranks[...] = rank_row
    slot_row = coded(row & 65535).astype(BF)
    for a, b in ((0, HP),):
        parts = []
        for c in range(a, b, 128):
            down = jnp.broadcast_to(rank_row[:, c : c + 128], (8, 128)).T
            vcol[c : c + 128, :] = jnp.broadcast_to(down[:, 0:1], (128, 128)).astype(BF)
            parts.append(
                jnp.where(slot_row[:, c : c + 128] == code_ref[...], jnp.ones((), BF), jnp.zeros((), BF))
            )
        part = jnp.concatenate(parts, axis=1)
        onehot[:, a:b] = part
        spread = jnp.dot(reach_ref[...], part, preferred_element_type=F32).astype(BF)
        for c in range(a, b, 128):
            part = spread[:, c - a : c - a + 128]
            left[:, c : c + 128] = part * show
            diag[:, c : c + 128] = part * fold
    cards = jnp.dot(diag[...], gather_ref[...], preferred_element_type=F32)
    high = cards.astype(BF).astype(F32)
    lane = lax.broadcasted_iota(jnp.int32, cards.shape, 1)
    left[:, HP:] = jnp.where(lane < 64, high, cards - high).astype(BF)


def settle(compat_ref, spread_ref, sums, vcol, onehot, left, diag, terms, ranks):
    rank_row = ranks[...].astype(BF)
    for a, b in pieces(HP):
        limit = compat_ref[:, a:b]
        gap = rank_row[:, a:b] - jnp.concatenate([vcol[...]] * ((b - a) // 128), axis=1)
        against = jnp.minimum(jnp.maximum(gap, -limit), limit)
        right = jnp.concatenate([against, spread_ref[:, a:b]], axis=0)
        chosen = jnp.dot(left[...], right, preferred_element_type=F32)
        chosen = chosen + diag[:, a:b].astype(F32)
        count = lax.broadcasted_iota(jnp.int32, chosen.shape, 0) == 0
        chosen = jnp.where(count, 1.0, chosen)
        high = chosen.astype(BF)
        terms[0 : 2 * S, a:b] = high
        terms[2 * S :, a:b] = (chosen - high.astype(F32)).astype(BF)
    for a, b in ((0, WIN),):
        got = lax.dot_general(
            terms[...], onehot[a:b, :], (((1,), (1,)), ((), ())), preferred_element_type=F32
        )
        sums[:, a:b] = sums[:, a:b] + got[: 2 * S] + got[2 * S :]


def board_kernel(
    there_ref, table_ref, boards, reach_ref, sigma_ref, show_ref, fold_ref, fixed_any,
    mine_ref, theirs_ref, compat_ref, gather_ref, spread_ref, code_ref,
    sums, value0, value1, mine_list, sems, *buffers,
):
    pairs = [(fixed_any.at[pl.ds(0, WIN), pl.ds(HP + EXT, 128)], code_ref),
             (fixed_any.at[pl.ds(0, HP), pl.ds(HP, EXT)], gather_ref),
             (fixed_any.at[pl.ds(HP, EXT), pl.ds(0, HP)], spread_ref)]
    for a, b in pieces(HP):
        pairs.append((fixed_any.at[pl.ds(0, HP), pl.ds(a, b - a)], compat_ref.at[:, pl.ds(a, b - a)]))
    copies = [pltpu.make_async_copy(a, b, sems.at[i]) for i, (a, b) in enumerate(pairs)]
    for copy in copies:
        copy.start()
    sums[...] = jnp.zeros(sums.shape, F32)
    seq, hand = lax.axis_index("seq"), lax.axis_index("hand")

    kept, seen = jnp.int32(0), hand
    for i in range(4 * there_ref.shape[0]):
        flag = there_ref[i // 4, i % 4]
        both = flag & 1
        mine_list[kept] = i
        kept = kept + (flag >> 1) + (both & (1 - (seen & 1)))
        seen = seen + both

    show = show_ref[...].astype(BF)
    fold = fold_ref[...].astype(BF)

    def deal(i, turn=0):
        vcol, onehot, left, diag, terms, ranks = buffers[6 * turn : 6 * turn + 6]
        index = mine_list[i]
        give(boards[index >> 2, pl.ds(index & 3, 1), :], reach_ref, show, fold, gather_ref, code_ref,
             vcol, onehot, left, diag, ranks)

    for copy in copies[:2]:
        copy.wait()
    deal(0)
    for copy in copies[2:]:
        copy.wait()

    def add(turn=0):
        settle(compat_ref, spread_ref, sums, *buffers[6 * turn : 6 * turn + 6])

    @pl.when(kept > 0)
    def _():
        add()

    def step(i, carry):
        for turn in range(2):
            deal(1 + 2 * i + turn, turn)
            add(turn)
        return carry

    left_over = jnp.maximum(kept - 1, 0)
    lax.fori_loop(0, left_over >> 1, step, 0)

    @pl.when((left_over & 1) == 1)
    def _():
        deal(kept - 1)
        add()

    value = (value0, value1)
    for p in range(2):
        for r in range(8):
            value[p][pl.ds(r, S, stride=8), :] = sums[p * S : p * S + S, 128 * r : 128 * r + 128]

    def at(s):
        return pl.ds(pl.multiple_of(8 * s, 8), 8)

    def put(place, tile):
        turned = jnp.concatenate([tile[4:], tile[:4]], axis=0)
        tile = jnp.where(hand == 0, tile, turned)
        mine_ref[place] = tile[:4]
        theirs_ref[place] = tile[4:]

    mass = value[0][0:8, :]
    for k in range(4):
        put((k, pl.ds(192, 4)), mass)
    value[0][0:8, :] = jnp.zeros((8, 128), F32)
    for s in range(1, S):
        scale = table_ref[2 * S + s].astype(F32) / H
        for p in range(2):
            value[p][8 * s : 8 * s + 8, :] = value[p][8 * s : 8 * s + 8, :] * scale
    for s in range(S - 1, 0, -1):
        up = at(table_ref[S + s])
        sigma = sigma_ref[8 * s : 8 * s + 8, :]
        actor = table_ref[s]
        for p in range(2):
            own = value[p][8 * s : 8 * s + 8, :]
            value[p][up, :] = value[p][up, :] + jnp.where(actor == p, sigma, 1.0) * own
    for s in range(S):
        chunk = jnp.bitwise_xor(seq, s // 16)
        row = 4 * (s % 16)
        for p in range(2):
            put((chunk, pl.ds(64 * p + row, 4)), value[p][8 * s : 8 * s + 8, :])
        if s == 0:
            put((chunk, pl.ds(128 + row, 4)), jnp.zeros((8, 128), F32))
        else:
            up = at(table_ref[S + s])
            actor = table_ref[s]
            own = jnp.where(actor == 0, value[0][8 * s : 8 * s + 8, :], value[1][8 * s : 8 * s + 8, :])
            over = jnp.where(actor == 0, value[0][up, :], value[1][up, :])
            put((chunk, pl.ds(128 + row, 4)), own - over)


def finish_kernel(logits_ref, mine, got, c1, c2, c3, new_ref, values_ref, total):
    total[...] = ((mine[0] + got[0]) + c1[...]) + (c2[...] + c3[...])
    for r in range(4):
        mass = total[192 + r : 193 + r, :] + 1.0
        lanes = slice(128 * r, 128 * r + 128)
        for p in range(2):
            values_ref[p, :, lanes] = total[pl.ds(64 * p + r, 16, stride=4), :] / mass
        gain = total[pl.ds(128 + r, 16, stride=4), :] / mass
        new_ref[:, lanes] = logits_ref[:, lanes] + STEP * gain


def swap(x, axis, size, bits):
    return lax.ppermute(x, axis, [(i, i ^ bits) for i in range(size)])


def local(board_cards, ranks, buckets, parent, action, pot, logits):
    sds = jax.ShapeDtypeStruct
    pair, fixed = constants()
    groups, planes = lax.axis_size("boards"), 8
    boards = board_cards.shape[0]
    slots = boards // planes
    other = swap(logits, "hand", 2, 1)
    own = pl.pallas_call(
        prep_kernel,
        compiler_params=pltpu.CompilerParams(vmem_limit_bytes=60 * 2**20),
        out_shape=sds((groups, slots, HP), jnp.int32),
        in_specs=[VM, VM, VM, VM],
        out_specs=VM,
        cost_estimate=pl.CostEstimate(flops=4_000_000_000, bytes_accessed=2_000_000, transcendentals=0),
        scratch_shapes=[pltpu.VMEM((boards, HQ), jnp.int32)],
    )(board_cards.T, ranks, buckets, jnp.asarray(pair))
    own, other = lax.optimization_barrier((own, other))
    wide = jnp.stack([logits, other])
    packs = lax.all_to_all(own, "boards", 0, 0)
    blocks = [wide] + [swap(wide, "seq", 4, k) for k in FAR_LAST]
    small = pltpu.CompilerParams(vmem_limit_bytes=8 * 2**20)
    show, fold, table = pl.pallas_call(
        tree_kernel,
        compiler_params=small,
        out_shape=[sds((2 * S, 128), F32), sds((2 * S, 128), F32), sds((3 * S,), jnp.int32)],
        in_specs=[SM] * 3 + [AN],
        out_specs=[VM, VM, SM],
        scratch_shapes=[pltpu.SMEM((S,), jnp.int32)] * 2,
        cost_estimate=pl.CostEstimate(flops=1_000_000_000, bytes_accessed=2_000_000, transcendentals=0),
    )(parent, action, pot, wide)
    reach, sigma = pl.pallas_call(
        reach_kernel,
        compiler_params=small,
        out_shape=[sds((2 * S, WIN), BF), sds((8 * S, 128), F32)],
        in_specs=[SM] + [VM] * 4,
        out_specs=[VM] * 2,
        scratch_shapes=[
            pltpu.VMEM((8 * S, 128), F32),
            *[pltpu.VMEM((4 * S, 128), F32)] * 5,
            *[pltpu.VMEM((8 * S, 128), F32)] * 2,
        ],
        cost_estimate=pl.CostEstimate(flops=4_000_000, bytes_accessed=2_000_000, transcendentals=65536),
    )(table, *blocks)
    there = packs[:, :, LIVE] >> 16
    mine, theirs = pl.pallas_call(
        board_kernel,
        out_shape=[sds((4, 200, 128), F32)] * 2,
        in_specs=[SM] * 2 + [VM] * 5 + [AN],
        out_specs=[VM] * 2,
        scratch_shapes=[
            pltpu.VMEM((HP, HP), BF),
            pltpu.VMEM((HP, EXT), BF),
            pltpu.VMEM((EXT, HP), BF),
            pltpu.VMEM((WIN, 128), BF),
            pltpu.VMEM((2 * S, WIN), F32),
            *[pltpu.VMEM((8 * S, 128), F32)] * 2,
            pltpu.SMEM((groups * slots + 8,), jnp.int32),
            pltpu.SemaphoreType.DMA((8,)),
            *[
                pltpu.VMEM((HP, 128), BF),
                pltpu.VMEM((WIN, HP), BF),
                pltpu.VMEM((2 * S, HP + EXT), BF),
                pltpu.VMEM((2 * S, HP), BF),
                pltpu.VMEM((4 * S, HP), BF),
                pltpu.VMEM((1, HP), F32),
            ]
            * 2,
        ],
        compiler_params=pltpu.CompilerParams(vmem_limit_bytes=50 * 2**20),
        cost_estimate=pl.CostEstimate(flops=8_000_000_000, bytes_accessed=8_000_000, transcendentals=0),
    )(there, table, packs, reach, sigma, show, fold, jnp.asarray(fixed))
    got = swap(theirs, "hand", 2, 1)
    chunks = [swap(mine[k] + got[k], "seq", 4, k) for k in FAR_LAST]
    new_logits, values = pl.pallas_call(
        finish_kernel,
        compiler_params=pltpu.CompilerParams(vmem_limit_bytes=8 * 2**20),
        out_shape=[sds(logits.shape, F32), sds((2,) + logits.shape, F32)],
        in_specs=[VM] * 6,
        out_specs=[VM] * 2,
        scratch_shapes=[pltpu.VMEM((200, 128), F32)],
    )(logits, mine, got, *chunks)
    return new_logits, values


def solution(mesh):
    return jax.shard_map(
        local,
        mesh=mesh,
        in_specs=(
            P("boards", None),
            P("boards", None),
            P("boards", None),
            P(),
            P(),
            P(),
            P("seq", ("boards", "hand")),
        ),
        out_specs=(P("seq", ("boards", "hand")), P(None, "seq", ("boards", "hand"))),
        check_vma=False,
    )
```

```python
import functools

import jax
import jax.numpy as jnp
import ml_dtypes
import numpy as np
from jax import lax
from jax.experimental import pallas as pl
from jax.experimental.pallas import tpu as pltpu
from jax.sharding import PartitionSpec as P

CARDS = 52
FREE = CARDS - 5
S = 64
WIN = 1024
H = CARDS * (CARDS - 1) // 2
LIVE = FREE * (FREE - 1) // 2
HQ = 1408
HP = 1152
EXT = 128
DEAD = 2047
STEP = 0.5
FAR_LAST = (1, 3, 2)
BF = jnp.bfloat16
F32 = jnp.float32
VM = pl.BlockSpec(memory_space=pltpu.VMEM)
SM = pl.BlockSpec(memory_space=pltpu.SMEM)
AN = pl.BlockSpec(memory_space=pl.ANY)


def constants():
    pair = np.full((2, HQ), CARDS, np.int32)
    pair[:, :H] = np.triu_indices(CARDS, 1)
    first, second = np.triu_indices(FREE, 1)
    held = np.zeros((HP, 64), np.float32)
    held[np.arange(LIVE), first] = 1
    held[np.arange(LIVE), second] = 1
    compat = np.zeros((HP, HP), np.float32)
    compat[:LIVE, :LIVE] = (held @ held.T)[:LIVE, :LIVE] == 0
    held[:LIVE, FREE] = 1
    gather = np.concatenate([held, held], axis=1)
    held[:, :FREE] *= -1
    spread = np.concatenate([held, held], axis=1).T
    k = np.arange(WIN)
    code = np.broadcast_to(((128 + k % 128) * 2.0 ** (k // 128))[:, None], (WIN, 128))
    code = np.pad(code, ((0, HP - WIN), (0, 0)))
    fixed = np.concatenate([compat, gather, code], axis=1)
    fixed = np.concatenate([fixed, np.pad(spread, ((0, 0), (0, EXT + 128)))], axis=0)
    return pair, np.asarray(fixed, ml_dtypes.bfloat16)


def coded(value):
    power = jnp.ones(value.shape, F32)
    for bit in range(6):
        on = (value >> (7 + bit)) & 1
        power = power * jnp.where(on == 1, float(2 ** (2**bit)), 1.0)
    return ((value & 127) + 128).astype(F32) * power


def prep_kernel(cards_ref, ranks_ref, buckets_ref, pair_ref, out_ref, wide):
    boards = buckets_ref.shape[0]
    wide[:, 0:H] = ranks_ref[...] * 2048 + (buckets_ref[...] & (WIN - 1))
    lanes = lax.broadcasted_iota(jnp.int32, (1, HQ), 1)
    row = lax.broadcasted_iota(jnp.int32, (boards, boards), 0)
    col = lax.broadcasted_iota(jnp.int32, (boards, boards), 1)

    def across(key):
        return jnp.sum(jnp.where(row == col, key.astype(F32), 0.0), axis=0, keepdims=True)

    def down(key):
        return jnp.sum(jnp.where(row == col, key.astype(F32), 0.0), axis=1, keepdims=True).astype(jnp.int32)

    first, second = pair_ref[0:1, :], pair_ref[1:2, :]
    low, high = first, second
    dead = lanes >= H
    for c in range(5):
        card = down(cards_ref[c : c + 1, :])
        dead = dead | (first == card) | (second == card)
        low = low - jnp.where(card < first, 1, 0)
        high = high - jnp.where(card < second, 1, 0)
    shift = lanes - (((low * (2 * FREE - 1 - low)) >> 1) + high - low - 1)
    word = jnp.where(dead, DEAD, (wide[...] & 0xFFFFFF) + (shift << 24))
    for bit in range(8):
        moved = pltpu.roll(word, HQ - (1 << bit), 1)
        mark = jnp.int32(-(2**31) if bit == 7 else 2 ** (24 + bit))
        word = jnp.where(moved & mark != 0, moved, jnp.where(word & mark != 0, DEAD, word))
    seq, hand = lax.axis_index("seq"), lax.axis_index("hand")
    group = lax.axis_index("boards")
    cluster = buckets_ref[:, 0:1] // WIN
    same = across(cluster) == cluster.astype(F32)

    def count(mask):
        return jnp.sum(jnp.where(mask, 1.0, 0.0), axis=1, keepdims=True).astype(jnp.int32)

    twins = count(same & (col < row))
    few = count(same) <= 16
    turn = cluster + (group >> 1) + twins
    ours = jnp.where(few, turn & 3, turn & 7) == jnp.where(few, seq, seq + 4 * hand)
    slots = out_ref.shape[1]
    slot = jnp.where(ours, slots * cluster + jnp.where(few, twins >> 2, twins >> 3), -1)
    flag = jnp.where(few, 1, 2)
    word = jnp.where(lanes[:, :HP] < LIVE, word[:, :HP] & 0xFFFFFF, 2048 * flag + DEAD)
    taken = lax.broadcasted_iota(jnp.int32, (slots * out_ref.shape[0], boards), 0).astype(F32) == across(slot)
    taken = jnp.where(taken, 1.0, 0.0).astype(BF)

    def deal(shift):
        part = ((word >> shift) & 255).astype(F32).astype(BF)
        return jnp.dot(taken, part, preferred_element_type=F32).astype(jnp.int32)

    word = deal(0) + (deal(8) << 8) + (deal(16) << 16)
    word = ((word >> 11) << 16) + (word & 2047)
    for c in range(out_ref.shape[0]):
        out_ref[c] = word[slots * c : slots * c + slots, :]


def tree_scalars(parent_ref, depth, inner):
    depth[0] = 0
    for s in range(S):
        inner[s] = 0
    for s in range(1, S):
        up = parent_ref[s]
        depth[s] = depth[up] + 1
        inner[up] = 1


def tree_kernel(parent_ref, action_ref, pot_ref, wide_any, show_ref, fold_ref, table_ref, depth, inner):
    tree_scalars(parent_ref, depth, inner)
    table_ref[0] = 1
    table_ref[S] = 0
    table_ref[2 * S] = 0
    zero = jnp.zeros((1, 128), F32)
    show_ref[0:1, :] = zero
    show_ref[S : S + 1, :] = zero
    fold_ref[0:1, :] = zero
    fold_ref[S : S + 1, :] = zero
    for s in range(1, S):
        actor = (depth[s] + 1) & 1
        table_ref[s] = actor
        table_ref[S + s] = parent_ref[s]
        table_ref[2 * S + s] = pot_ref[s]
        leaf = 1 - inner[s]
        folds = jnp.where(action_ref[s] == 0, leaf, 0)
        shows = (leaf - folds).astype(F32)
        folds = folds.astype(F32)
        for p in range(2):
            show_ref[p * S + s : p * S + s + 1, :] = jnp.full((1, 128), shows, F32)
            sign = jnp.where(actor == p, -folds, folds)
            fold_ref[p * S + s : p * S + s + 1, :] = jnp.full((1, 128), sign, F32)


def reach_kernel(table_ref, *refs):
    blocks = refs[:4]
    reach_ref, sigma_ref = refs[4:6]
    line, parts, top, reach = refs[6], refs[7:11], refs[11], refs[12:14]
    seq, hand = lax.axis_index("seq"), lax.axis_index("hand")
    for k, block in zip((0,) + FAR_LAST, blocks):
        base = 128 * jnp.bitwise_xor(seq, k)
        for half in range(2):
            start = base + 4 * jnp.bitwise_xor(hand, half)
            for r in range(4):
                line[pl.ds(start + r, 16, stride=8), :] = block[
                    half, :, 128 * r : 128 * r + 128
                ]

    def at(s):
        return pl.ds(pl.multiple_of(8 * s, 8), 8)

    for part in parts:
        part[...] = jnp.full(part.shape, -jnp.inf, F32)
    for s in range(1, S):
        part, up = parts[s % 4], at(table_ref[S + s])
        part[up, :] = jnp.maximum(part[up, :], line[8 * s : 8 * s + 8, :])
    top[...] = jnp.maximum(
        jnp.maximum(parts[0][...], parts[1][...]), jnp.maximum(parts[2][...], parts[3][...])
    )
    for part in parts:
        part[...] = jnp.zeros(part.shape, F32)
    for s in range(1, S):
        part, up = parts[s % 4], at(table_ref[S + s])
        raised = jnp.exp(line[8 * s : 8 * s + 8, :] - top[up, :])
        sigma_ref[8 * s : 8 * s + 8, :] = raised
        part[up, :] = part[up, :] + raised
    top[...] = (parts[0][...] + parts[1][...]) + (parts[2][...] + parts[3][...])
    one = jnp.ones((8, 128), F32)
    sigma_ref[0:8, :] = one
    for p in range(2):
        reach[p][0:8, :] = one
    for s in range(1, S):
        up = at(table_ref[S + s])
        sigma = sigma_ref[8 * s : 8 * s + 8, :] / top[up, :]
        sigma_ref[8 * s : 8 * s + 8, :] = sigma
        actor = table_ref[s]
        for p in range(2):
            weight = jnp.where(actor == p, sigma, one)
            reach[p][8 * s : 8 * s + 8, :] = weight * reach[p][up, :]
    for p in range(2):
        for r in range(8):
            reach_ref[p * S : p * S + S, 128 * r : 128 * r + 128] = reach[1 - p][
                pl.ds(r, S, stride=8), :
            ].astype(BF)


def pieces(width):
    return [(a, min(a + 256, width)) for a in range(0, width, 256)]


def give(row, reach_ref, show, fold, gather_ref, code_ref, vcol, onehot, left, diag, ranks):
    rank_row = coded(row >> 16)
    ranks[...] = rank_row
    slot_row = coded(row & 65535).astype(BF)
    for a, b in ((0, HP),):
        parts = []
        for c in range(a, b, 128):
            down = jnp.broadcast_to(rank_row[:, c : c + 128], (8, 128)).T
            vcol[c : c + 128, :] = jnp.broadcast_to(down[:, 0:1], (128, 128)).astype(BF)
            parts.append(
                jnp.where(slot_row[:, c : c + 128] == code_ref[...], jnp.ones((), BF), jnp.zeros((), BF))
            )
        part = jnp.concatenate(parts, axis=1)
        onehot[:, a:b] = part
        spread = jnp.dot(reach_ref[...], part, preferred_element_type=F32).astype(BF)
        for c in range(a, b, 128):
            part = spread[:, c - a : c - a + 128]
            left[:, c : c + 128] = part * show
            diag[:, c : c + 128] = part * fold
    cards = jnp.dot(diag[...], gather_ref[...], preferred_element_type=F32)
    high = cards.astype(BF).astype(F32)
    lane = lax.broadcasted_iota(jnp.int32, cards.shape, 1)
    left[:, HP:] = jnp.where(lane < 64, high, cards - high).astype(BF)


def settle(compat_ref, spread_ref, sums, vcol, onehot, left, diag, terms, ranks):
    rank_row = ranks[...].astype(BF)
    for a, b in pieces(HP):
        limit = compat_ref[:, a:b]
        gap = rank_row[:, a:b] - jnp.concatenate([vcol[...]] * ((b - a) // 128), axis=1)
        against = jnp.minimum(jnp.maximum(gap, -limit), limit)
        right = jnp.concatenate([against, spread_ref[:, a:b]], axis=0)
        chosen = jnp.dot(left[...], right, preferred_element_type=F32)
        chosen = chosen + diag[:, a:b].astype(F32)
        count = lax.broadcasted_iota(jnp.int32, chosen.shape, 0) == 0
        chosen = jnp.where(count, 1.0, chosen)
        high = chosen.astype(BF)
        terms[0 : 2 * S, a:b] = high
        terms[2 * S :, a:b] = (chosen - high.astype(F32)).astype(BF)
    for a, b in ((0, WIN),):
        got = lax.dot_general(
            terms[...], onehot[a:b, :], (((1,), (1,)), ((), ())), preferred_element_type=F32
        )
        sums[:, a:b] = sums[:, a:b] + got[: 2 * S] + got[2 * S :]


def board_kernel(
    there_ref, table_ref, boards, reach_ref, sigma_ref, show_ref, fold_ref, fixed_any,
    mine_ref, theirs_ref, compat_ref, gather_ref, spread_ref, code_ref,
    sums, value0, value1, mine_list, sems, share0, share1, share2, share3, *buffers,
):
    pairs = [(fixed_any.at[pl.ds(0, WIN), pl.ds(HP + EXT, 128)], code_ref),
             (fixed_any.at[pl.ds(0, HP), pl.ds(HP, EXT)], gather_ref),
             (fixed_any.at[pl.ds(HP, EXT), pl.ds(0, HP)], spread_ref)]
    for a, b in pieces(HP):
        pairs.append((fixed_any.at[pl.ds(0, HP), pl.ds(a, b - a)], compat_ref.at[:, pl.ds(a, b - a)]))
    copies = [pltpu.make_async_copy(a, b, sems.at[i]) for i, (a, b) in enumerate(pairs)]
    for copy in copies:
        copy.start()
    sums[...] = jnp.zeros(sums.shape, F32)
    seq, hand = lax.axis_index("seq"), lax.axis_index("hand")

    kept, seen = jnp.int32(0), hand
    for i in range(4 * there_ref.shape[0]):
        flag = there_ref[i // 4, i % 4]
        both = flag & 1
        mine_list[kept] = i
        kept = kept + (flag >> 1) + (both & (1 - (seen & 1)))
        seen = seen + both

    show = show_ref[...].astype(BF)
    fold = fold_ref[...].astype(BF)

    def deal(i, turn=0):
        vcol, onehot, left, diag, terms, ranks = buffers[6 * turn : 6 * turn + 6]
        index = mine_list[i]
        give(boards[index >> 2, pl.ds(index & 3, 1), :], reach_ref, show, fold, gather_ref, code_ref,
             vcol, onehot, left, diag, ranks)

    for copy in copies[:2]:
        copy.wait()
    deal(0)
    for copy in copies[2:]:
        copy.wait()

    def add(turn=0):
        settle(compat_ref, spread_ref, sums, *buffers[6 * turn : 6 * turn + 6])

    @pl.when(kept > 0)
    def _():
        add()

    def step(i, carry):
        for turn in range(2):
            deal(1 + 2 * i + turn, turn)
            add(turn)
        return carry

    left_over = jnp.maximum(kept - 1, 0)
    lax.fori_loop(0, left_over >> 1, step, 0)

    @pl.when((left_over & 1) == 1)
    def _():
        deal(kept - 1)
        add()

    value = (value0, value1)
    shares = (share0, share1, share2, share3)
    for p in range(2):
        for r in range(8):
            value[p][pl.ds(r, S, stride=8), :] = sums[p * S : p * S + S, 128 * r : 128 * r + 128]

    def at(s):
        return pl.ds(pl.multiple_of(8 * s, 8), 8)

    def put(place, tile):
        turned = jnp.concatenate([tile[4:], tile[:4]], axis=0)
        tile = jnp.where(hand == 0, tile, turned)
        mine_ref[place] = tile[:4]
        theirs_ref[place] = tile[4:]

    mass = value[0][0:8, :]
    for k in range(4):
        put((k, pl.ds(192, 4)), mass)
    value[0][0:8, :] = jnp.zeros((8, 128), F32)
    for s in range(1, S):
        scale = table_ref[2 * S + s].astype(F32) / H
        for p in range(2):
            value[p][8 * s : 8 * s + 8, :] = value[p][8 * s : 8 * s + 8, :] * scale
    for part in shares:
        part[...] = jnp.zeros(part.shape, F32)
    for s in range(S // 2, S):
        up = at(table_ref[S + s])
        sigma = sigma_ref[8 * s : 8 * s + 8, :]
        actor = table_ref[s]
        for p in range(2):
            part = shares[2 * p + s % 2]
            own = value[p][8 * s : 8 * s + 8, :]
            part[up, :] = part[up, :] + jnp.where(actor == p, sigma, 1.0) * own
    for p in range(2):
        value[p][0 : 4 * S, :] = value[p][0 : 4 * S, :] + (shares[2 * p][...] + shares[2 * p + 1][...])
    for s in range(S // 2 - 1, 0, -1):
        up = at(table_ref[S + s])
        sigma = sigma_ref[8 * s : 8 * s + 8, :]
        actor = table_ref[s]
        for p in range(2):
            own = value[p][8 * s : 8 * s + 8, :]
            value[p][up, :] = value[p][up, :] + jnp.where(actor == p, sigma, 1.0) * own
    for s in range(S):
        chunk = jnp.bitwise_xor(seq, s // 16)
        row = 4 * (s % 16)
        for p in range(2):
            put((chunk, pl.ds(64 * p + row, 4)), value[p][8 * s : 8 * s + 8, :])
        if s == 0:
            put((chunk, pl.ds(128 + row, 4)), jnp.zeros((8, 128), F32))
        else:
            up = at(table_ref[S + s])
            actor = table_ref[s]
            own = jnp.where(actor == 0, value[0][8 * s : 8 * s + 8, :], value[1][8 * s : 8 * s + 8, :])
            over = jnp.where(actor == 0, value[0][up, :], value[1][up, :])
            put((chunk, pl.ds(128 + row, 4)), own - over)


def finish_kernel(logits_ref, mine, got, c1, c2, c3, new_ref, values_ref, total):
    total[...] = ((mine[0] + got[0]) + c1[...]) + (c2[...] + c3[...])
    for r in range(4):
        mass = total[192 + r : 193 + r, :] + 1.0
        lanes = slice(128 * r, 128 * r + 128)
        for p in range(2):
            values_ref[p, :, lanes] = total[pl.ds(64 * p + r, 16, stride=4), :] / mass
        gain = total[pl.ds(128 + r, 16, stride=4), :] / mass
        new_ref[:, lanes] = logits_ref[:, lanes] + STEP * gain


def swap(x, axis, size, bits):
    return lax.ppermute(x, axis, [(i, i ^ bits) for i in range(size)])


def local(board_cards, ranks, buckets, parent, action, pot, logits):
    sds = jax.ShapeDtypeStruct
    pair, fixed = constants()
    groups, planes = lax.axis_size("boards"), 8
    boards = board_cards.shape[0]
    slots = boards // planes
    other = swap(logits, "hand", 2, 1)
    own = pl.pallas_call(
        prep_kernel,
        compiler_params=pltpu.CompilerParams(vmem_limit_bytes=60 * 2**20),
        out_shape=sds((groups, slots, HP), jnp.int32),
        in_specs=[VM, VM, VM, VM],
        out_specs=VM,
        cost_estimate=pl.CostEstimate(flops=4_000_000_000, bytes_accessed=2_000_000, transcendentals=0),
        scratch_shapes=[pltpu.VMEM((boards, HQ), jnp.int32)],
    )(board_cards.T, ranks, buckets, jnp.asarray(pair))
    own, other = lax.optimization_barrier((own, other))
    wide = jnp.stack([logits, other])
    packs = lax.all_to_all(own, "boards", 0, 0)
    blocks = [wide] + [swap(wide, "seq", 4, k) for k in FAR_LAST]
    small = pltpu.CompilerParams(vmem_limit_bytes=8 * 2**20)
    show, fold, table = pl.pallas_call(
        tree_kernel,
        compiler_params=small,
        out_shape=[sds((2 * S, 128), F32), sds((2 * S, 128), F32), sds((3 * S,), jnp.int32)],
        in_specs=[SM] * 3 + [AN],
        out_specs=[VM, VM, SM],
        scratch_shapes=[pltpu.SMEM((S,), jnp.int32)] * 2,
        cost_estimate=pl.CostEstimate(flops=1_000_000_000, bytes_accessed=2_000_000, transcendentals=0),
    )(parent, action, pot, wide)
    reach, sigma = pl.pallas_call(
        reach_kernel,
        compiler_params=small,
        out_shape=[sds((2 * S, WIN), BF), sds((8 * S, 128), F32)],
        in_specs=[SM] + [VM] * 4,
        out_specs=[VM] * 2,
        scratch_shapes=[
            pltpu.VMEM((8 * S, 128), F32),
            *[pltpu.VMEM((4 * S, 128), F32)] * 5,
            *[pltpu.VMEM((8 * S, 128), F32)] * 2,
        ],
        cost_estimate=pl.CostEstimate(flops=4_000_000, bytes_accessed=2_000_000, transcendentals=65536),
    )(table, *blocks)
    there = packs[:, :, LIVE] >> 16
    mine, theirs = pl.pallas_call(
        board_kernel,
        out_shape=[sds((4, 200, 128), F32)] * 2,
        in_specs=[SM] * 2 + [VM] * 5 + [AN],
        out_specs=[VM] * 2,
        scratch_shapes=[
            pltpu.VMEM((HP, HP), BF),
            pltpu.VMEM((HP, EXT), BF),
            pltpu.VMEM((EXT, HP), BF),
            pltpu.VMEM((WIN, 128), BF),
            pltpu.VMEM((2 * S, WIN), F32),
            *[pltpu.VMEM((8 * S, 128), F32)] * 2,
            pltpu.SMEM((groups * slots + 8,), jnp.int32),
            pltpu.SemaphoreType.DMA((8,)),
            *[pltpu.VMEM((4 * S, 128), F32)] * 4,
            *[
                pltpu.VMEM((HP, 128), BF),
                pltpu.VMEM((WIN, HP), BF),
                pltpu.VMEM((2 * S, HP + EXT), BF),
                pltpu.VMEM((2 * S, HP), BF),
                pltpu.VMEM((4 * S, HP), BF),
                pltpu.VMEM((1, HP), F32),
            ]
            * 2,
        ],
        compiler_params=pltpu.CompilerParams(vmem_limit_bytes=50 * 2**20),
        cost_estimate=pl.CostEstimate(flops=8_000_000_000, bytes_accessed=8_000_000, transcendentals=0),
    )(there, table, packs, reach, sigma, show, fold, jnp.asarray(fixed))
    got = swap(theirs, "hand", 2, 1)
    chunks = [swap(mine[k] + got[k], "seq", 4, k) for k in FAR_LAST]
    new_logits, values = pl.pallas_call(
        finish_kernel,
        compiler_params=pltpu.CompilerParams(vmem_limit_bytes=8 * 2**20),
        out_shape=[sds(logits.shape, F32), sds((2,) + logits.shape, F32)],
        in_specs=[VM] * 6,
        out_specs=[VM] * 2,
        scratch_shapes=[pltpu.VMEM((200, 128), F32)],
    )(logits, mine, got, *chunks)
    return new_logits, values


def solution(mesh):
    return jax.shard_map(
        local,
        mesh=mesh,
        in_specs=(
            P("boards", None),
            P("boards", None),
            P("boards", None),
            P(),
            P(),
            P(),
            P("seq", ("boards", "hand")),
        ),
        out_specs=(P("seq", ("boards", "hand")), P(None, "seq", ("boards", "hand"))),
        check_vma=False,
    )
```
